256 devices in a mesh: rows: 64 (over z, y_hi, x), slab: 4 (over y_lo, core).
Axes of the slice: x: 4, y: 4 (y_hi: 2, y_lo: 2; y = y_hi * 2 + y_lo), z: 8, core: 2. Of those that a mesh axis runs over, the one named last changes fastest.
Arguments:
- adj_tiles: bfloat16 [12288, 128, 128], P('rows'), may hold values from 0.0019073486 to 0.030517578
- tile_index: int32 [12288, 2], P('rows'), may hold values from 0 to 255, as said below
- grad_out: bfloat16 [32768, 256], P('rows', 'slab'), may hold values from -6 to 6
- relu_mask: int32 [32768, 256], P('rows', 'slab'), may hold values 0 or 1
- features: bfloat16 [32768, 256], P('rows'), may hold values from -0.09375 to 0.09375
- weight: bfloat16 [256, 256], P(None, 'slab'), may hold values from -0.375 to 0.375
Outputs:
- grad_input: bfloat16 [32768, 256], P('rows', 'slab')
- grad_weight: float32 [256, 256], P('rows', 'slab')
The draws below stay inside these ranges and needn't reach their ends.
Inputs may be any that keep to these rules, and one draw needn't show every extreme that they name: `tile_index`: row t of a list on index d of rows (rows d * 192 to (d + 1) * 192 - 1) holds a row block in d's own range d * 4 to (d + 1) * 4 - 1 and a column block whose owner (column block // 4) never falls along the list; no list holds more than 12 tiles of one owner, and every list holds exactly 12 tiles of some owner.
All inputs are finite; a program needn't handle non-finite values. No bound on the sum of `relu_mask` on one device may be relied on, other than what follows from the above.
Results may differ from the reference program's by a relative error of at most 0.015.
Values may be sent and summed in bfloat16 or wider, within the bound.
No kernel may reach another device: no remote copies, remote signals or barrier semaphores. Data moves between devices by JAX's collectives and lax.ppermute only.
A program may use at most 64 MiB of HBM per device.

```python
import math
import jax
import jax.numpy as jnp
from jax import lax

C = 256
TILE = 128
BLOCKS_DEV = 4
NODES = 32768
TILES_DEV = 192
TILES = 12288
MAX_TILES_PER_ROW = 12
N_ROWS = 64


def one_list(key, device):
    keys = jax.random.split(key, 4)
    others = N_ROWS - 1
    leftover = TILES_DEV - MAX_TILES_PER_ROW
    minimum_count = leftover // others
    surplus_count = leftover % others
    heaviest_rows = jax.random.randint(keys[0], (), 0, N_ROWS)
    shuffled = jax.random.permutation(keys[1], N_ROWS)
    load_ranking = jnp.argsort(shuffled).astype(jnp.int32)
    load_ranking = load_ranking - (load_ranking > load_ranking[heaviest_rows]).astype(jnp.int32)
    owning_devices = jnp.arange(N_ROWS, dtype=jnp.int32)
    additional_tile = ((load_ranking < surplus_count) & (owning_devices != heaviest_rows)).astype(jnp.int32)
    tile_counts = jnp.where(owning_devices == heaviest_rows, MAX_TILES_PER_ROW, minimum_count + additional_tile).astype(jnp.int32)
    ends = jnp.cumsum(tile_counts)
    places = jnp.arange(TILES_DEV, dtype=jnp.int32)
    source = jnp.sum((ends[None, :] <= places[:, None]).astype(jnp.int32), axis=1)
    column = source * BLOCKS_DEV + jax.random.randint(keys[2], (TILES_DEV,), 0, BLOCKS_DEV)
    row_block = device * BLOCKS_DEV + jax.random.randint(keys[3], (TILES_DEV,), 0, BLOCKS_DEV)
    return jnp.stack([row_block, column], axis=1).astype(jnp.int32)


def draw_tile_index(key, part):
    key = jax.random.fold_in(key, 7)
    device_keys = jax.random.split(key, N_ROWS)
    lists = jax.vmap(one_list)(device_keys, jnp.arange(N_ROWS, dtype=jnp.int32))
    return lists.reshape(TILES, 2)


def set_ends(values, own_key, smallest, largest):
    shape = values.shape
    spot = [jax.random.randint(jax.random.fold_in(own_key, axis), (), 0, shape[axis]) for axis in range(len(shape))]
    values = values.at[tuple(spot)].set(smallest)
    longest = shape.index(max(shape))
    spot[longest] = (spot[longest] + 1) % shape[longest]
    return values.at[tuple(spot)].set(largest)


def with_spikes(drawn, rng, source, target, parts, factor):
    def block_of(dim):
        return (jnp.arange(drawn.shape[dim]) // (drawn.shape[dim] // parts)).reshape((-1,) + (1,) * (drawn.ndim - 1 - dim))

    near = jax.random.permutation(rng, parts)[block_of(target)]
    second = (block_of(target) + parts // 2) % parts
    return jnp.where((block_of(source) == near) | (block_of(source) == second), factor * drawn, drawn)


def block_scale(stream_key, extent, pieces, low, largest):
    level = 1.0
    for dim, blocks in pieces:
        heights = jax.random.uniform(jax.random.fold_in(jax.random.fold_in(stream_key, 6), dim), (blocks,), jnp.float32, low / len(pieces), largest / len(pieces))
        level = level * jnp.repeat(jnp.exp(heights), extent[dim] // blocks).reshape((-1,) + (1,) * (len(extent) - 1 - dim))
    return level


def gaussian(stream_key, shape, spread, limit, cuts=(), kind=jnp.bfloat16):
    values = spread * jax.random.normal(stream_key, shape, jnp.float32)
    if cuts:
        values = values * block_scale(stream_key, shape, cuts, -0.22, 0.18)
    return jnp.clip(values, -limit, limit).astype(kind)


def heavy_noise(own_key, extent, deviation, bound, shards, heavy, held_as=jnp.bfloat16):
    array = deviation * jax.random.normal(own_key, extent, jnp.float32)
    if shards:
        array = array * block_scale(own_key, extent, shards, -0.22, 0.18)
    return jnp.clip(with_spikes(array, jax.random.fold_in(own_key, 3), *heavy), -bound, bound).astype(held_as)


def setup_inputs(seed: int = 0) -> dict:
    arg_keys = jax.random.split(jax.random.key(seed), 7)
    return {
        "adj_tiles": jnp.clip(jnp.exp(math.log(0.030517578) - 2.7725887 * jax.random.uniform(arg_keys[0], (TILES, TILE, TILE), jnp.float32) ** block_scale(arg_keys[0], (TILES, TILE, TILE), ((0, 64),), -0.2, 0.2)), 0.0019073486, 0.030517578).astype(jnp.bfloat16),
        "tile_index": draw_tile_index(jax.random.fold_in(arg_keys[6], 71), 0),
        "grad_out": gaussian(arg_keys[2], (NODES, C), 1.0, 6.0, ((0, 64), (1, 4))),
        "relu_mask": set_ends((jax.random.randint(arg_keys[3], (NODES, C), 0, 2) < 1).astype(jnp.int32), jax.random.fold_in(arg_keys[3], 1), 0, 1),
        "features": heavy_noise(arg_keys[4], (NODES, C), NODES ** -0.5, 0.09375, ((0, 64),), (0, 1, 64, 4.0)),
        "weight": gaussian(arg_keys[5], (C, C), C ** -0.5, 0.375, ((1, 4),)),
    }


def reference(adj_tiles, tile_index, grad_out, relu_mask, features, weight):
    g_pre = (grad_out.astype(jnp.float32) * relu_mask.astype(jnp.float32)).astype(jnp.bfloat16)
    count_blocks = NODES // TILE
    blocks = g_pre.reshape(count_blocks, TILE, C).astype(jnp.float32)
    tiles = adj_tiles.reshape(N_ROWS, TILES_DEV, TILE, TILE)
    entries = tile_index.reshape(N_ROWS, TILES_DEV, 2)

    def add_tiles(totals, item):
        values, where_at = item
        picked = blocks[where_at[:, 1]]
        products = jnp.einsum("tij,tjc->tic", values.astype(jnp.float32), picked, precision=lax.Precision.HIGHEST)
        return totals.at[where_at[:, 0]].add(products), None

    start = jnp.zeros((count_blocks, TILE, C), jnp.float32)
    agg, unused = lax.scan(add_tiles, start, (tiles, entries))
    agg_b = agg.reshape(NODES, C).astype(jnp.bfloat16)
    grad_input = jnp.dot(agg_b, weight.T, preferred_element_type=jnp.float32).astype(jnp.bfloat16)
    grad_weight = jnp.dot(features.T, agg_b, preferred_element_type=jnp.float32)
    return grad_input, grad_weight
```

```python
import jax
import jax.numpy as jnp
from jax import lax
from jax.experimental import pallas as pl
from jax.experimental.pallas import tpu as pltpu
from jax.sharding import Mesh, PartitionSpec as P

ROWS = ("z", "yh", "x")
SLAB = ("yl", "core")
GROUP = 8


def tile_table(tile_index, first_row, block_slot, steps):
    listed = tile_index.shape[0]
    row = tile_index[:, 0] - first_row
    slot, half = block_slot(tile_index[:, 1])
    t = jnp.arange(listed)
    rank = jnp.sum(((row[None, :] == row[:, None]) & (t[None, :] < t[:, None])).astype(jnp.int32), axis=1)
    r4 = jnp.arange(4)
    count = jnp.sum((row[:, None] == r4[None, :]).astype(jnp.int32), axis=0)
    need = (count + GROUP - 1) // GROUP
    ends = jnp.sum(jnp.where(r4[None, :] <= r4[:, None], need[None, :], 0), axis=1)
    starts = ends - need
    place = jnp.sum(jnp.where(row[:, None] == r4[None, :], starts[None, :], 0), axis=1) * GROUP + rank
    value = 1 + t + slot * 256 + half * 65536
    j = jnp.arange(steps * GROUP)
    table = jnp.sum(jnp.where(place[None, :] == j[:, None], value[None, :], 0), axis=1)
    table = jnp.where(table > 0, table - 1, 2 * 65536)
    step_row = jnp.minimum(jnp.sum((ends[None, :] <= jnp.arange(steps)[:, None]).astype(jnp.int32), axis=1), 3)
    return table.astype(jnp.int32), jnp.concatenate([step_row, ends[3:]]).astype(jnp.int32)


def agg_kernel(table, step_row, adj, blocks, out, acc, masks):
    steps = step_row.shape[0] - 1
    lane = lax.broadcasted_iota(jnp.int32, (128, 128), 1)
    masks[0] = jnp.where(lane < 64, 1.0, 0.0).astype(masks.dtype)
    masks[1] = jnp.where(lane < 64, 0.0, 1.0).astype(masks.dtype)
    masks[2] = jnp.zeros((128, 128), masks.dtype)
    acc[...] = jnp.zeros_like(acc)

    def step(s, carry):
        lhs, rhs = [], []
        for u in range(GROUP):
            e = table[s * GROUP + u]
            lhs.append(adj[e & 255])
            rhs.append(blocks[(e >> 8) & 255] * masks[e >> 16])
        acc[step_row[s]] += jnp.dot(
            jnp.concatenate(lhs, axis=1), jnp.concatenate(rhs, axis=0), preferred_element_type=jnp.float32
        )
        return carry

    lax.fori_loop(0, step_row[steps], step, 0)
    agg = [acc[r] + pltpu.roll(acc[r], 64, 1) for r in range(4)]
    for r in range(2):
        out[pl.ds(r * 128, 128), :] = jnp.where(lane < 64, agg[r], agg[r + 2]).astype(out.dtype)


def aggregate(table, step_row, adj, blocks):
    smem = pl.BlockSpec(memory_space=pltpu.SMEM)
    vmem = pl.BlockSpec(memory_space=pltpu.VMEM)
    return pl.pallas_call(
        agg_kernel,
        out_shape=jax.ShapeDtypeStruct((256, 128), jnp.bfloat16),
        in_specs=[smem, smem, vmem, vmem],
        out_specs=vmem,
        scratch_shapes=[pltpu.VMEM((4, 128, 128), jnp.float32), pltpu.VMEM((3, 128, 128), jnp.bfloat16)],
        compiler_params=pltpu.CompilerParams(vmem_limit_bytes=32 * 1024 * 1024),
        name="aggregate",
    )(table, step_row, adj, blocks)


def halves(packed):
    return jnp.concatenate([packed[:, :64], packed[:, 64:]], axis=0)


def body(adj_tiles, tile_index, grad_out, relu_mask, features, weight):
    position = lax.axis_index(ROWS)
    slab = lax.axis_index(SLAB)
    g_pre = (grad_out.astype(jnp.float32) * relu_mask.astype(jnp.float32)).astype(jnp.bfloat16)
    packed = jnp.concatenate([g_pre[:256], g_pre[256:]], axis=1)

    flips = ([(0, 1), (1, 0), (2, 3), (3, 2)], [(0, 2), (2, 0), (1, 3), (3, 1)], [(0, 3), (3, 0), (1, 2), (2, 1)])
    w_parts = [lax.dynamic_slice_in_dim(weight, slab * 64, 64, 0)]
    for k, pairs in enumerate(flips):
        w_parts.append(lax.ppermute(lax.dynamic_slice_in_dim(weight, (slab ^ (k + 1)) * 64, 64, 0), SLAB, pairs))

    gathered = lax.all_gather(packed, "yh", axis=0, tiled=False)
    gathered = lax.all_gather(gathered, "x", axis=0, tiled=False)
    gathered = lax.all_gather(gathered, "z", axis=0, tiled=False)

    def block_slot(column):
        owner, block = column // 4, column % 4
        z, y, x = owner // 8, (owner // 4) % 2, owner % 4
        return ((z * 4 + x) * 2 + y) * 2 + block % 2, block // 2

    steps = adj_tiles.shape[0] // GROUP + 4
    table, step_row = tile_table(tile_index, position * 4, block_slot, steps)
    agg = aggregate(table, step_row, adj_tiles, gathered.reshape(128, 128, 128))

    a_parts = [halves(agg)] + [halves(lax.ppermute(agg, SLAB, pairs)) for pairs in flips]
    grad_input = jnp.einsum(
        "rs,is->ri", jnp.concatenate(a_parts, axis=1), jnp.concatenate(w_parts, axis=1), preferred_element_type=jnp.float32
    ).astype(jnp.bfloat16)

    partial = jnp.einsum("ri,rs->is", features, a_parts[0], preferred_element_type=jnp.float32)
    pieces = lax.all_to_all(partial.reshape(64, 256), ROWS, 0, 0, tiled=True)
    grad_weight = jnp.sum(pieces, axis=0).reshape(4, 64)
    return grad_input, grad_weight


def solution(mesh):
    fine = Mesh(mesh.devices.reshape(8, 2, 4, 2, 2), ROWS + SLAB)
    return jax.shard_map(
        body,
        mesh=fine,
        in_specs=(P(ROWS, None, None), P(ROWS, None), P(ROWS, SLAB), P(ROWS, SLAB), P(ROWS, None), P(None, SLAB)),
        out_specs=(P(ROWS, SLAB), P(ROWS, SLAB)),
        check_vma=False,
    )
```

```python
import jax
import jax.numpy as jnp
from jax import lax
from jax.experimental import pallas as pl
from jax.experimental.pallas import tpu as pltpu
from jax.sharding import Mesh, PartitionSpec as P

NZ, NY, NX, NL, NC = 8, 2, 4, 2, 2
ROWS = ("z", "yh", "x")
SLAB = ("yl", "core")
ALL = ROWS + SLAB
GROUP = 8
SLOTS = 4
FLIPS = ([(0, 1), (1, 0), (2, 3), (3, 2)], [(0, 2), (2, 0), (1, 3), (3, 1)], [(0, 3), (3, 0), (1, 2), (2, 1)])


def device(z, y, x, l, c):
    return ((((z % NZ) * NY + y % NY) * NX + x % NX) * NL + l) * NC + c


def places():
    return [(z, y, x, l, c) for z in range(NZ) for y in range(NY) for x in range(NX) for l in range(NL) for c in range(NC)]


def from_rows(value, dz=0, dy=0):
    pairs = [(device(z + dz, y + dy, x, l, c), device(z, y, x, l, c)) for z, y, x, l, c in places()]
    return lax.ppermute(value, ALL, pairs)


def from_axis(value, second, step):
    pairs = []
    for z, y, x, l, c in places():
        along_x = (c == 0) != second
        source = device(z, y, x + step, l, c) if along_x else device(z + step, y, x, l, c)
        pairs.append((source, device(z, y, x, l, c)))
    return lax.ppermute(value, ALL, pairs)


def gather_near(packed):
    four = jnp.stack([packed, from_rows(packed, dy=1), from_rows(packed, dz=4), from_rows(packed, dz=4, dy=1)])
    early = jnp.stack([four, from_axis(four, False, 1), from_axis(four, False, -1), from_axis(four, False, 2)])
    plus, minus = from_axis(early, True, 1), from_axis(early, True, -1)
    return early, plus, minus


def gather_far(plus, minus):
    return [from_axis(plus[:2], True, 1), from_axis(minus[2:], True, -1)]


def where_held(column):
    owner, block = column // 4, column % 4
    core = lax.axis_index("core")
    dz = (owner // (NY * NX) - lax.axis_index("z")) % NZ
    dy = (owner // NX - lax.axis_index("yh")) % NY
    dx = (owner - lax.axis_index("x")) % NX
    ring = jnp.where(core == 0, dx, dz % 4)
    late = jnp.where(core == 0, dz % 4, dx)
    a = jnp.where(ring == 2, 3, jnp.where(ring == 3, 2, ring))
    upper = (dz >= 3) & (dz <= 6)
    swapped = (core == 0) & (late == 2) & (a >= 2)
    e = dy + 2 * (upper != swapped).astype(jnp.int32)
    stage = jnp.where(late == 0, 0, jnp.where(late == 2, 2, 1))
    place = (a * 4 + e) * 2 + block % 2 + jnp.where(late == 3, 32, 0)
    return stage, place, block // 2


def tile_table(row, valid, place, half, steps):
    t = jnp.arange(row.shape[0])
    row = jnp.where(valid, row, -1)
    r4 = jnp.arange(4)
    rank = jnp.sum(((row[None, :] == row[:, None]) & (t[None, :] < t[:, None])).astype(jnp.int32), axis=1)
    count = jnp.sum((row[:, None] == r4[None, :]).astype(jnp.int32), axis=0)
    need = (count + GROUP - 1) // GROUP
    ends = jnp.sum(jnp.where(r4[None, :] <= r4[:, None], need[None, :], 0), axis=1)
    starts = ends - need
    slot = jnp.sum(jnp.where(row[:, None] == r4[None, :], starts[None, :], 0), axis=1) * GROUP + rank
    slot = jnp.where(valid, slot, -1)
    value = 1 + t + place * 256 + half * 65536
    j = jnp.arange(steps * GROUP)
    table = jnp.sum(jnp.where(slot[None, :] == j[:, None], value[None, :], 0), axis=1)
    table = jnp.where(table > 0, table - 1, 2 * 65536)
    step_row = jnp.minimum(jnp.sum((ends[None, :] <= jnp.arange(steps)[:, None]).astype(jnp.int32), axis=1), 3)
    return table.astype(jnp.int32), jnp.concatenate([step_row, ends[3:]]).astype(jnp.int32)


def add_tiles(table, step_row, adj, sources, acc, blocks, tiles, masks, block_sems, tile_sems):
    steps = step_row[step_row.shape[0] - 1]
    each = blocks.shape[0] // len(sources)
    copies = [
        pltpu.make_async_copy(src, blocks.at[pl.ds(k * each, each)], block_sems.at[k]) for k, src in enumerate(sources)
    ]
    for copy in copies:
        copy.start()

    def fetch(s):
        slot = lax.rem(s, SLOTS)
        for u in range(GROUP):
            pltpu.make_async_copy(adj.at[table[s * GROUP + u] & 255], tiles.at[slot, u], tile_sems.at[slot]).start()

    for s in range(SLOTS - 1):
        @pl.when(s < steps)
        def _():
            fetch(s)

    lane = lax.broadcasted_iota(jnp.int32, (128, 128), 1)
    masks[0] = jnp.where(lane < 64, 1.0, 0.0).astype(masks.dtype)
    masks[1] = jnp.where(lane < 64, 0.0, 1.0).astype(masks.dtype)
    masks[2] = jnp.zeros((128, 128), masks.dtype)
    for copy in copies:
        copy.wait()

    def step(s, carry):
        @pl.when(s + SLOTS - 1 < steps)
        def _():
            fetch(s + SLOTS - 1)

        slot = lax.rem(s, SLOTS)
        pltpu.make_async_copy(adj.at[pl.ds(0, GROUP)], tiles.at[slot], tile_sems.at[slot]).wait()
        lhs, rhs = [], []
        for u in range(GROUP):
            e = table[s * GROUP + u]
            lhs.append(tiles[slot, u])
            rhs.append(blocks[(e >> 8) & 255] * masks[e >> 16])
        acc[step_row[s]] += jnp.dot(
            jnp.concatenate(lhs, axis=1), jnp.concatenate(rhs, axis=0), preferred_element_type=jnp.float32
        )
        return carry

    lax.fori_loop(0, steps, step, 0)
    return lane


def pre_kernel(grad_out, relu_mask, out):
    g = grad_out[...].astype(jnp.float32) * relu_mask[...].astype(jnp.float32)
    out[...] = jnp.concatenate([g[:, :256], g[:, 256:]], axis=0).T.astype(out.dtype)


def masked(grad_out, relu_mask):
    vmem = pl.BlockSpec(memory_space=pltpu.VMEM)
    return pl.pallas_call(
        pre_kernel,
        out_shape=jax.ShapeDtypeStruct((256, 128), jnp.bfloat16),
        in_specs=[vmem, vmem],
        out_specs=vmem,
        name="masked",
    )(grad_out.T, relu_mask.T)


def first_kernel(table, step_row, adj, source, acc, *scratch):
    acc[...] = jnp.zeros_like(acc)
    add_tiles(table, step_row, adj, [source], acc, *scratch)


def middle_kernel(table, step_row, adj, source_a, source_b, before, acc, *scratch):
    acc[...] = before[...]
    add_tiles(table, step_row, adj, [source_a, source_b], acc, *scratch)


def last_kernel(table, step_row, adj, source_a, source_b, before, features, out, partial, acc, *scratch):
    acc[...] = before[...]
    lane = add_tiles(table, step_row, adj, [source_a, source_b], acc, *scratch)
    agg = [acc[r] + pltpu.roll(acc[r], 64, 1) for r in range(4)]
    for r in range(2):
        out[pl.ds(r * 128, 128), :] = jnp.where(lane < 64, agg[r], agg[r + 2]).astype(out.dtype)
    rounded = jnp.concatenate([v.astype(jnp.bfloat16) for v in agg], axis=0)
    product = jnp.dot(features[...], rounded, preferred_element_type=jnp.float32)
    low = lax.broadcasted_iota(jnp.int32, (64, 128), 1) < 64
    for p in range(2):
        partial[:, p, :] = jnp.where(low, product[p * 128 : p * 128 + 64], product[p * 128 + 64 : p * 128 + 128])


def call(kernel, table, step_row, adj, sources, others, out_shape, keep_acc, name):
    smem = pl.BlockSpec(memory_space=pltpu.SMEM)
    vmem = pl.BlockSpec(memory_space=pltpu.VMEM)
    anywhere = pl.BlockSpec(memory_space=pl.ANY)
    sources = [s.reshape(-1, 128, 128) for s in sources]
    held = sum(s.shape[0] for s in sources)
    return pl.pallas_call(
        kernel,
        out_shape=out_shape,
        in_specs=[smem, smem, anywhere] + [anywhere] * len(sources) + [vmem] * len(others),
        out_specs=jax.tree.map(lambda _: vmem, out_shape),
        scratch_shapes=([pltpu.VMEM((4, 128, 128), jnp.float32)] if keep_acc else []) + [
            pltpu.VMEM((held, 128, 128), jnp.bfloat16),
            pltpu.VMEM((SLOTS, GROUP, 128, 128), jnp.bfloat16),
            pltpu.VMEM((3, 128, 128), jnp.bfloat16),
            pltpu.SemaphoreType.DMA((len(sources),)),
            pltpu.SemaphoreType.DMA((SLOTS,)),
        ],
        compiler_params=pltpu.CompilerParams(vmem_limit_bytes=16 * 1024 * 1024),
        cost_estimate=pl.CostEstimate(flops=2 * 64 * 128 * 128 * 128, bytes_accessed=8 * 1024 * 1024, transcendentals=0),
        name=name,
    )(table, step_row, adj, *sources, *others)


def halves(packed):
    return jnp.concatenate([packed[:, :64], packed[:, 64:]], axis=0)


def body(adj_tiles, tile_index, grad_out, relu_mask, features, weight):
    position = lax.axis_index(ROWS)
    slab = lax.axis_index(SLAB)
    early, plus, minus = gather_near(masked(grad_out, relu_mask))

    steps = adj_tiles.shape[0] // GROUP + 4
    stage, place, half = where_held(tile_index[:, 1])
    row = tile_index[:, 0] - position * 4
    tables = [tile_table(row, stage == k, place, half, steps) for k in range(3)]
    f_rows = features.reshape(512, 64, 4).transpose(2, 1, 0).reshape(256, 512)

    sums = jax.ShapeDtypeStruct((4, 128, 128), jnp.float32)
    acc = call(first_kernel, *tables[0], adj_tiles, [early], [], sums, False, "early_tiles")
    weight, acc, plus, minus, f_rows, tables = lax.optimization_barrier((weight, acc, plus, minus, f_rows, tables))
    far = gather_far(plus, minus)
    w_parts = [lax.dynamic_slice_in_dim(weight, slab * 64, 64, 0)]
    for k, pairs in enumerate(FLIPS):
        w_parts.append(lax.ppermute(lax.dynamic_slice_in_dim(weight, (slab ^ (k + 1)) * 64, 64, 0), SLAB, pairs))
    acc = call(middle_kernel, *tables[1], adj_tiles, [plus, minus], [acc], sums, False, "near_tiles")
    outs = (jax.ShapeDtypeStruct((256, 128), jnp.bfloat16), jax.ShapeDtypeStruct((64, 2, 128), jnp.float32))
    agg, partial = call(last_kernel, *tables[2], adj_tiles, far, [acc, f_rows], outs, True, "far_tiles")

    pieces = lax.all_to_all(partial, ROWS, 0, 0, tiled=True)
    a_parts = [halves(agg)] + [halves(lax.ppermute(agg, SLAB, pairs)) for pairs in FLIPS]
    grad_input = jnp.einsum(
        "rs,is->ri", jnp.concatenate(a_parts, axis=1), jnp.concatenate(w_parts, axis=1), preferred_element_type=jnp.float32
    ).astype(jnp.bfloat16)
    grad_weight = jnp.sum(pieces, axis=0).reshape(4, 64)
    return grad_input, grad_weight


def solution(mesh):
    fine = Mesh(mesh.devices.reshape(NZ, NY, NX, NL, NC), ALL)
    return jax.shard_map(
        body,
        mesh=fine,
        in_specs=(P(ROWS, None, None), P(ROWS, None), P(ROWS, SLAB), P(ROWS, SLAB), P(ROWS, None), P(None, SLAB)),
        out_specs=(P(ROWS, SLAB), P(ROWS, SLAB)),
        check_vma=False,
    )
```

```python
import jax
import jax.numpy as jnp
from jax import lax
from jax.experimental import pallas as pl
from jax.experimental.pallas import tpu as pltpu
from jax.sharding import Mesh, PartitionSpec as P

NZ, NY, NX, NL, NC = 8, 2, 4, 2, 2
ROWS = ("z", "yh", "x")
SLAB = ("yl", "core")
ALL = ROWS + SLAB
GROUP = 4
FLIPS = ([(0, 1), (1, 0), (2, 3), (3, 2)], [(0, 2), (2, 0), (1, 3), (3, 1)], [(0, 3), (3, 0), (1, 2), (2, 1)])


def device(z, y, x, l, c):
    return ((((z % NZ) * NY + y % NY) * NX + x % NX) * NL + l) * NC + c


def places():
    return [(z, y, x, l, c) for z in range(NZ) for y in range(NY) for x in range(NX) for l in range(NL) for c in range(NC)]


def from_rows(value, dz=0, dy=0):
    pairs = [(device(z + dz, y + dy, x, l, c), device(z, y, x, l, c)) for z, y, x, l, c in places()]
    return lax.ppermute(value, ALL, pairs)


def from_axis(value, second, step):
    pairs = []
    for z, y, x, l, c in places():
        along_x = (c == 0) != second
        z_step = -step if step == 2 and z % 2 else step
        source = device(z, y, x + step, l, c) if along_x else device(z + z_step, y, x, l, c)
        pairs.append((source, device(z, y, x, l, c)))
    return lax.ppermute(value, ALL, pairs)


def gather_near(packed):
    far_y, far = from_rows(packed, dz=4, dy=1), from_rows(packed, dz=4)
    four = jnp.stack([packed, from_rows(again(packed), dy=1), far, far_y])
    early = jnp.stack([four, from_axis(four, False, 1), from_axis(four, False, -1), from_axis(four, False, 2)])
    plus, minus = from_axis(early, True, 1), from_axis(early, True, -1)
    return early, plus, minus


def gather_far(plus, minus):
    return [from_axis(plus[:2], True, 1), from_axis(minus[2:], True, -1)]


def where_held(column):
    owner, block = column // 4, column % 4
    core = lax.axis_index("core")
    dz = (owner // (NY * NX) - lax.axis_index("z")) % NZ
    dy = (owner // NX - lax.axis_index("yh")) % NY
    dx = (owner - lax.axis_index("x")) % NX
    ring = jnp.where(core == 0, dx, dz % 4)
    late = jnp.where(core == 0, dz % 4, dx)
    a = jnp.where(ring == 2, 3, jnp.where(ring == 3, 2, ring))
    upper = (dz >= 3) & (dz <= 6)
    swapped = jnp.where(core == 0, (late == 2) & (a >= 2), (ring == 2) & (lax.axis_index("z") % 2 == 1))
    e = dy + 2 * (upper != swapped).astype(jnp.int32)
    source = jnp.where(late == 0, 0, jnp.where(late == 1, 1, jnp.where(late == 3, 2, 3 + a // 2)))
    place = (jnp.where(late == 2, a % 2, a) * 4 + e) * 2 + block % 2
    return source, place, block // 2


def tile_table(row, source, place, half, count):
    listed = row.shape[0]
    t = jnp.arange(listed)
    r4, sources = jnp.arange(4), jnp.arange(count)
    key = source * 4 + row
    rank = jnp.sum(((key[None, :] == key[:, None]) & (t[None, :] < t[:, None])).astype(jnp.int32), axis=1)
    held = jnp.sum((key[:, None] == jnp.arange(count * 4)[None, :]).astype(jnp.int32), axis=0).reshape(count, 4)
    need = jnp.max((held + GROUP - 1) // GROUP, axis=1)
    bounds = jnp.sum(jnp.where(sources[None, :] < jnp.arange(count + 1)[:, None], need[None, :], 0), axis=1)
    begin = jnp.sum(jnp.where(source[:, None] == sources[None, :], bounds[None, :count], 0), axis=1)
    slot = ((begin + rank // GROUP) * 4 + row) * GROUP + rank % GROUP
    value = 1 + t + place * 256 + half * 65536
    j = jnp.arange((listed // GROUP + count) * 4 * GROUP)
    table = jnp.sum(jnp.where(slot[None, :] == j[:, None], value[None, :], 0), axis=1)
    return jnp.where(table > 0, table - 1, 2 * 65536).astype(jnp.int32), bounds.astype(jnp.int32)


def add_tiles(table, first, last, adj, blocks, acc, masks):
    def step(s, carry):
        for r in range(4):
            lhs, rhs = [], []
            for u in range(GROUP):
                e = table[(s * 4 + r) * GROUP + u]
                lhs.append(adj[e & 255])
                rhs.append(blocks[(e >> 8) & 255] * masks[e >> 16])
            acc[r] += jnp.dot(
                jnp.concatenate(lhs, axis=1), jnp.concatenate(rhs, axis=0), preferred_element_type=jnp.float32
            )
        return carry

    lax.fori_loop(first, last, step, 0)


def set_masks(masks):
    lane = lax.broadcasted_iota(jnp.int32, (128, 128), 1)
    masks[0] = jnp.where(lane < 64, 1.0, 0.0).astype(masks.dtype)
    masks[1] = jnp.where(lane < 64, 0.0, 1.0).astype(masks.dtype)
    masks[2] = jnp.zeros((128, 128), masks.dtype)
    return lane


def pre_kernel(grad_out, relu_mask, out):
    g = grad_out[...].astype(jnp.float32) * relu_mask[...].astype(jnp.float32)
    out[...] = jnp.concatenate([g[:, :256], g[:, 256:]], axis=0).T.astype(out.dtype)


def masked(grad_out, relu_mask):
    vmem = pl.BlockSpec(memory_space=pltpu.VMEM)
    return pl.pallas_call(
        pre_kernel,
        out_shape=jax.ShapeDtypeStruct((256, 128), jnp.bfloat16),
        in_specs=[vmem, vmem],
        out_specs=vmem,
        name="masked",
    )(grad_out.T, relu_mask.T)


def again_kernel(value, out):
    out[...] = value[...]


def again(value):
    vmem = pl.BlockSpec(memory_space=pltpu.VMEM)
    shape = jax.ShapeDtypeStruct(value.shape, value.dtype)
    return pl.pallas_call(again_kernel, out_shape=shape, in_specs=[vmem], out_specs=vmem, name="again")(value)


def first_kernel(table, bounds, adj, source, acc, masks):
    set_masks(masks)
    acc[...] = jnp.zeros_like(acc)
    add_tiles(table, bounds[0], bounds[1], adj, source, acc, masks)


def middle_kernel(table, bounds, adj, source_a, source_b, before, acc, masks):
    set_masks(masks)
    acc[...] = before[...]
    add_tiles(table, bounds[1], bounds[2], adj, source_a, acc, masks)
    add_tiles(table, bounds[2], bounds[3], adj, source_b, acc, masks)


def last_kernel(table, bounds, adj, source_a, source_b, before, features, out, partial, acc, masks):
    lane = set_masks(masks)
    acc[...] = before[...]
    add_tiles(table, bounds[3], bounds[4], adj, source_a, acc, masks)
    add_tiles(table, bounds[4], bounds[5], adj, source_b, acc, masks)
    agg = [acc[r] + pltpu.roll(acc[r], 64, 1) for r in range(4)]
    for r in range(2):
        out[pl.ds(r * 128, 128), :] = jnp.where(lane < 64, agg[r], agg[r + 2]).astype(out.dtype)
    rounded = jnp.concatenate([v.astype(jnp.bfloat16) for v in agg], axis=0)
    product = jnp.dot(features[...], rounded, preferred_element_type=jnp.float32)
    low = lax.broadcasted_iota(jnp.int32, (64, 128), 1) < 64
    for p in range(2):
        partial[:, p, :] = jnp.where(low, product[p * 128 : p * 128 + 64], product[p * 128 + 64 : p * 128 + 128])


def call(kernel, table, bounds, adj, sources, others, out_shape, keep_acc, name):
    smem = pl.BlockSpec(memory_space=pltpu.SMEM)
    vmem = pl.BlockSpec(memory_space=pltpu.VMEM)
    sources = [s.reshape(-1, 128, 128) for s in sources]
    return pl.pallas_call(
        kernel,
        out_shape=out_shape,
        in_specs=[smem, smem, vmem] + [vmem] * len(sources) + [vmem] * len(others),
        out_specs=jax.tree.map(lambda _: vmem, out_shape),
        scratch_shapes=([pltpu.VMEM((4, 128, 128), jnp.float32)] if keep_acc else []) + [
            pltpu.VMEM((3, 128, 128), jnp.bfloat16),
        ],
        compiler_params=pltpu.CompilerParams(vmem_limit_bytes=24 * 1024 * 1024),
        cost_estimate=pl.CostEstimate(flops=2 * 64 * 128 * 128 * 128, bytes_accessed=8 * 1024 * 1024, transcendentals=0),
        name=name,
    )(table, bounds, adj, *sources, *others)


def halves(packed):
    return jnp.concatenate([packed[:, :64], packed[:, 64:]], axis=0)


def body(adj_tiles, tile_index, grad_out, relu_mask, features, weight):
    position = lax.axis_index(ROWS)
    slab = lax.axis_index(SLAB)
    early, plus, minus = gather_near(masked(grad_out, relu_mask))

    source, place, half = where_held(tile_index[:, 1])
    tables = tile_table(tile_index[:, 0] - position * 4, source, place, half, 5)
    f_rows = features.reshape(512, 64, 4).transpose(2, 1, 0).reshape(256, 512)

    sums = jax.ShapeDtypeStruct((4, 128, 128), jnp.float32)
    acc = call(first_kernel, *tables, adj_tiles, [early], [], sums, False, "early_tiles")
    weight, acc, plus, minus, f_rows, tables = lax.optimization_barrier((weight, acc, plus, minus, f_rows, tables))
    far = gather_far(plus, minus)
    w_parts = [lax.dynamic_slice_in_dim(weight, slab * 64, 64, 0)]
    for k, pairs in enumerate(FLIPS):
        w_parts.append(lax.ppermute(lax.dynamic_slice_in_dim(weight, (slab ^ (k + 1)) * 64, 64, 0), SLAB, pairs))
    acc = call(middle_kernel, *tables, adj_tiles, [plus, minus], [acc], sums, False, "near_tiles")
    outs = (jax.ShapeDtypeStruct((256, 128), jnp.bfloat16), jax.ShapeDtypeStruct((64, 2, 128), jnp.float32))
    agg, partial = call(last_kernel, *tables, adj_tiles, far, [acc, f_rows], outs, True, "far_tiles")

    pieces = lax.all_to_all(partial, ROWS, 0, 0, tiled=True)
    a_parts = [halves(agg)] + [halves(lax.ppermute(agg, SLAB, pairs)) for pairs in FLIPS]
    grad_input = jnp.einsum(
        "rs,is->ri", jnp.concatenate(a_parts, axis=1), jnp.concatenate(w_parts, axis=1), preferred_element_type=jnp.float32
    ).astype(jnp.bfloat16)
    grad_weight = jnp.sum(pieces, axis=0).reshape(4, 64)
    return grad_input, grad_weight


def solution(mesh):
    fine = Mesh(mesh.devices.reshape(NZ, NY, NX, NL, NC), ALL)
    return jax.shard_map(
        body,
        mesh=fine,
        in_specs=(P(ROWS, None, None), P(ROWS, None), P(ROWS, SLAB), P(ROWS, SLAB), P(ROWS, None), P(None, SLAB)),
        out_specs=(P(ROWS, SLAB), P(ROWS, SLAB)),
        check_vma=False,
    )
```

```python
import jax
import jax.numpy as jnp
from jax import lax
from jax.experimental import pallas as pl
from jax.experimental.pallas import tpu as pltpu
from jax.sharding import Mesh, PartitionSpec as P

NZ, NY, NX, NL, NC = 8, 2, 4, 2, 2
ROWS = ("z", "yh", "x")
SLAB = ("yl", "core")
ALL = ROWS + SLAB
GROUP = 4
FLIPS = ([(0, 1), (1, 0), (2, 3), (3, 2)], [(0, 2), (2, 0), (1, 3), (3, 1)], [(0, 3), (3, 0), (1, 2), (2, 1)])


def device(z, y, x, l, c):
    return ((((z % NZ) * NY + y % NY) * NX + x % NX) * NL + l) * NC + c


def places():
    return [(z, y, x, l, c) for z in range(NZ) for y in range(NY) for x in range(NX) for l in range(NL) for c in range(NC)]


def from_rows(value, dz=0, dy=0):
    pairs = [(device(z + dz, y + dy, x, l, c), device(z, y, x, l, c)) for z, y, x, l, c in places()]
    return lax.ppermute(value, ALL, pairs)


def from_axis(value, second, step):
    pairs = []
    for z, y, x, l, c in places():
        along_x = (c == 0) != second
        z_step = -step if step == 2 and z % 2 else step
        source = device(z, y, x + step, l, c) if along_x else device(z + z_step, y, x, l, c)
        pairs.append((source, device(z, y, x, l, c)))
    return lax.ppermute(value, ALL, pairs)


def exchange(value, second_pairs):
    pairs = []
    for z, y, x, l, c in places():
        at = z if c == 0 else x
        step = 1 if (at % 2 == 0) != second_pairs else -1
        source = device(z + step, y, x, l, c) if c == 0 else device(z, y, x + step, l, c)
        pairs.append((source, device(z, y, x, l, c)))
    return lax.ppermute(value, ALL, pairs)


def odd_place():
    return jnp.where(lax.axis_index("core") == 0, lax.axis_index("z"), lax.axis_index("x")) % 2 == 1


def gather_early(packed, later):
    far_y, far = from_rows(packed, dz=4, dy=1), from_rows(packed, dz=4)
    again, later = lax.optimization_barrier((packed, later))
    four = jnp.stack([packed, from_rows(again, dy=1), far, far_y])
    low = jnp.stack([four, from_axis(four, False, 1)])
    high = jnp.stack([from_axis(four, False, -1), from_axis(four, False, 2)])
    return low, high, later


def gather_near(low, high):
    odd = odd_place()
    forwarded = [from_axis(low, True, 1), from_axis(high, True, -1)]
    low, high = lax.optimization_barrier((low, high))
    others = [exchange(jnp.where(odd, high, low), False), exchange(jnp.where(odd, low, high), True)]
    return forwarded, others


def gather_far(plus, minus):
    return [from_axis(plus, True, 1), from_axis(minus, True, -1)]


def where_held(column):
    owner, block = column // 4, column % 4
    core = lax.axis_index("core")
    dz = (owner // (NY * NX) - lax.axis_index("z")) % NZ
    dy = (owner // NX - lax.axis_index("yh")) % NY
    dx = (owner - lax.axis_index("x")) % NX
    ring = jnp.where(core == 0, dx, dz % 4)
    late = jnp.where(core == 0, dz % 4, dx)
    a = jnp.where(ring == 2, 3, jnp.where(ring == 3, 2, ring))
    upper = (dz >= 3) & (dz <= 6)
    swapped = jnp.where(core == 0, (late == 2) & (a >= 2), (ring == 2) & (lax.axis_index("z") % 2 == 1))
    e = dy + 2 * (upper != swapped).astype(jnp.int32)
    high, odd = a // 2, odd_place().astype(jnp.int32)
    after = jnp.where(high == 0, 2, 4 + odd)
    before = jnp.where(high == 1, 3, 5 - odd)
    source = jnp.where(late == 0, high, jnp.where(late == 1, after, jnp.where(late == 3, before, 6 + high)))
    place = (a % 2 * 4 + e) * 2 + block % 2
    return source, place, block // 2


def tile_table(row, source, place, half, count):
    listed = row.shape[0]
    t = jnp.arange(listed)
    r4, sources = jnp.arange(4), jnp.arange(count)
    key = source * 4 + row
    rank = jnp.sum(((key[None, :] == key[:, None]) & (t[None, :] < t[:, None])).astype(jnp.int32), axis=1)
    held = jnp.sum((key[:, None] == jnp.arange(count * 4)[None, :]).astype(jnp.int32), axis=0).reshape(count, 4)
    need = jnp.max((held + GROUP - 1) // GROUP, axis=1)
    bounds = jnp.sum(jnp.where(sources[None, :] < jnp.arange(count + 1)[:, None], need[None, :], 0), axis=1)
    begin = jnp.sum(jnp.where(source[:, None] == sources[None, :], bounds[None, :count], 0), axis=1)
    slot = ((begin + rank // GROUP) * 4 + row) * GROUP + rank % GROUP
    value = 1 + t + place * 256 + half * 65536
    j = jnp.arange((listed // GROUP + count) * 4 * GROUP)
    table = jnp.sum(jnp.where(slot[None, :] == j[:, None], value[None, :], 0), axis=1)
    return jnp.where(table > 0, table - 1, 2 * 65536).astype(jnp.int32), bounds.astype(jnp.int32)


def add_tiles(table, first, last, adj, blocks, acc, masks):
    def step(s, carry):
        for r in range(4):
            lhs, rhs = [], []
            for u in range(GROUP):
                e = table[(s * 4 + r) * GROUP + u]
                lhs.append(adj[e & 255])
                rhs.append(blocks[(e >> 8) & 255] * masks[e >> 16])
            acc[r] += jnp.dot(
                jnp.concatenate(lhs, axis=1), jnp.concatenate(rhs, axis=0), preferred_element_type=jnp.float32
            )
        return carry

    lax.fori_loop(first, last, step, 0)


def set_masks(masks):
    lane = lax.broadcasted_iota(jnp.int32, (128, 128), 1)
    masks[0] = jnp.where(lane < 64, 1.0, 0.0).astype(masks.dtype)
    masks[1] = jnp.where(lane < 64, 0.0, 1.0).astype(masks.dtype)
    masks[2] = jnp.zeros((128, 128), masks.dtype)
    return lane


def pre_kernel(grad_out, relu_mask, out):
    g = grad_out[...].astype(jnp.float32) * relu_mask[...].astype(jnp.float32)
    out[...] = jnp.concatenate([g[:, :256], g[:, 256:]], axis=0).T.astype(out.dtype)


def masked(grad_out, relu_mask):
    vmem = pl.BlockSpec(memory_space=pltpu.VMEM)
    return pl.pallas_call(
        pre_kernel,
        out_shape=jax.ShapeDtypeStruct((256, 128), jnp.bfloat16),
        in_specs=[vmem, vmem],
        out_specs=vmem,
        name="masked",
    )(grad_out.T, relu_mask.T)


def add_sources(table, bounds, adj, sources, first, acc, masks):
    for k, source in enumerate(sources):
        add_tiles(table, bounds[first + k], bounds[first + k + 1], adj, source, acc, masks)


def first_kernel(table, bounds, adj, *refs):
    *sources, acc, kept, masks = refs
    set_masks(masks)
    acc[...] = jnp.zeros_like(acc)
    add_sources(table, bounds, adj, sources, 0, acc, masks)


def middle_kernel(table, bounds, adj, *refs):
    *sources, before, acc, masks = refs
    set_masks(masks)
    acc[...] = before[...]
    add_sources(table, bounds, adj, sources, 2, acc, masks)


def last_kernel(table, bounds, adj, *refs):
    *sources, before, features, weights, out, out_a, out_b, out_c, partial, acc, masks = refs
    lane = set_masks(masks)
    acc[...] = before[...]
    add_sources(table, bounds, adj, sources, 6, acc, masks)
    agg = [acc[r] + pltpu.roll(acc[r], 64, 1) for r in range(4)]
    rounded = jnp.concatenate([v.astype(jnp.bfloat16) for v in agg], axis=0)
    product = jnp.dot(features[...], rounded, preferred_element_type=jnp.float32)
    low = lax.broadcasted_iota(jnp.int32, (64, 128), 1) < 64
    for p in range(2):
        partial[:, p, :] = jnp.where(low, product[p * 128 : p * 128 + 64], product[p * 128 + 64 : p * 128 + 128])
    for r in range(2):
        packed = jnp.where(lane < 64, agg[r], agg[r + 2]).astype(out.dtype)
        for ref in (out, out_a, out_b, out_c):
            ref[pl.ds(r * 128, 128), :] = packed
    for k, ref in enumerate((out_a, out_b, out_c)):
        ref[pl.ds(256, 64), :] = weights[k]


def call(kernel, table, bounds, adj, sources, others, out_shape, keep_acc, name, aliases={}):
    smem = pl.BlockSpec(memory_space=pltpu.SMEM)
    vmem = pl.BlockSpec(memory_space=pltpu.VMEM)
    sources = [s.reshape(-1, 128, 128) for s in sources]
    return pl.pallas_call(
        kernel,
        out_shape=out_shape,
        in_specs=[smem, smem, vmem] + [vmem] * len(sources) + [vmem] * len(others),
        out_specs=jax.tree.map(lambda _: vmem, out_shape),
        scratch_shapes=([pltpu.VMEM((4, 128, 128), jnp.float32)] if keep_acc else []) + [
            pltpu.VMEM((3, 128, 128), jnp.bfloat16),
        ],
        compiler_params=pltpu.CompilerParams(vmem_limit_bytes=8 * 1024 * 1024),
        cost_estimate=pl.CostEstimate(flops=2 * 64 * 128 * 128 * 128, bytes_accessed=8 * 1024 * 1024, transcendentals=0),
        input_output_aliases=aliases,
        name=name,
    )(table, bounds, adj, *sources, *others)


def halves(packed):
    return jnp.concatenate([packed[:, :64], packed[:, 64:]], axis=0)


def body(adj_tiles, tile_index, grad_out, relu_mask, features, weight):
    position = lax.axis_index(ROWS)
    slab = lax.axis_index(SLAB)
    source, place, half = where_held(tile_index[:, 1])
    low, high, source = gather_early(masked(grad_out, relu_mask), source)
    forwarded, others = gather_near(low, high)

    tables = tile_table(tile_index[:, 0] - position * 4, source, place, half, 8)
    f_rows = features.reshape(512, 64, 4).transpose(2, 1, 0).reshape(256, 512)
    w_parts = [lax.dynamic_slice_in_dim(weight, (slab ^ k) * 64, 64, 0) for k in range(4)]
    w_sent = jnp.pad(jnp.stack(w_parts[1:]), ((0, 0), (0, 0), (0, 64)))

    sums = jax.ShapeDtypeStruct((4, 128, 128), jnp.float32)
    kept = jax.ShapeDtypeStruct(adj_tiles.shape, adj_tiles.dtype)
    acc, adj = call(first_kernel, *tables, adj_tiles, [low, high], [], (sums, kept), False, "early_tiles", {2: 1})
    forwarded, acc, f_rows, w_sent = lax.optimization_barrier((forwarded, acc, f_rows, w_sent))
    far = gather_far(*forwarded)
    acc = call(middle_kernel, *tables, adj, forwarded + others, [acc], sums, False, "near_tiles")
    message = jax.ShapeDtypeStruct((320, 128), jnp.bfloat16)
    outs = (jax.ShapeDtypeStruct((256, 128), jnp.bfloat16), message, message, message, jax.ShapeDtypeStruct((64, 2, 128), jnp.float32))
    agg, *messages, partial = call(last_kernel, *tables, adj, far, [acc, f_rows, w_sent], outs, True, "far_tiles")

    pieces = lax.all_to_all(partial, ROWS, 0, 0, tiled=True)
    arrived = [lax.ppermute(m, SLAB, pairs) for m, pairs in zip(messages, FLIPS)]
    a_all = jnp.concatenate([halves(agg)] + [halves(m[:256]) for m in arrived], axis=1)
    w_all = jnp.concatenate([w_parts[0]] + [m[256:, :64] for m in arrived], axis=1)
    grad_input = jnp.einsum("rs,is->ri", a_all, w_all, preferred_element_type=jnp.float32).astype(jnp.bfloat16)
    grad_weight = jnp.sum(pieces, axis=0).reshape(4, 64)
    return grad_input, grad_weight


def solution(mesh):
    fine = Mesh(mesh.devices.reshape(NZ, NY, NX, NL, NC), ALL)
    return jax.shard_map(
        body,
        mesh=fine,
        in_specs=(P(ROWS, None, None), P(ROWS, None), P(ROWS, SLAB), P(ROWS, SLAB), P(ROWS, None), P(None, SLAB)),
        out_specs=(P(ROWS, SLAB), P(ROWS, SLAB)),
        check_vma=False,
    )
```

```python
import jax
import jax.numpy as jnp
from jax import lax
from jax.experimental import pallas as pl
from jax.experimental.pallas import tpu as pltpu
from jax.sharding import Mesh, PartitionSpec as P

NZ, NY, NX, NL, NC = 8, 2, 4, 2, 2
ROWS = ("z", "yh", "x")
SLAB = ("yl", "core")
ALL = ROWS + SLAB
GROUP = 4
FLIPS = ([(0, 1), (1, 0), (2, 3), (3, 2)], [(0, 2), (2, 0), (1, 3), (3, 1)], [(0, 3), (3, 0), (1, 2), (2, 1)])


def device(z, y, x, l, c):
    return ((((z % NZ) * NY + y % NY) * NX + x % NX) * NL + l) * NC + c


def places():
    return [(z, y, x, l, c) for z in range(NZ) for y in range(NY) for x in range(NX) for l in range(NL) for c in range(NC)]


def from_rows(value, dz=0, dy=0):
    pairs = [(device(z + dz, y + dy, x, l, c), device(z, y, x, l, c)) for z, y, x, l, c in places()]
    return lax.ppermute(value, ALL, pairs)


def from_axis(value, second, step):
    pairs = []
    for z, y, x, l, c in places():
        along_x = (c == 0) != second
        z_step = -step if step == 2 and z % 2 else step
        source = device(z, y, x + step, l, c) if along_x else device(z + z_step, y, x, l, c)
        pairs.append((source, device(z, y, x, l, c)))
    return lax.ppermute(value, ALL, pairs)


def exchange(value, second_pairs):
    pairs = []
    for z, y, x, l, c in places():
        at = z if c == 0 else x
        step = 1 if (at % 2 == 0) != second_pairs else -1
        source = device(z + step, y, x, l, c) if c == 0 else device(z, y, x + step, l, c)
        pairs.append((source, device(z, y, x, l, c)))
    return lax.ppermute(value, ALL, pairs)


def odd_place():
    return jnp.where(lax.axis_index("core") == 0, lax.axis_index("z"), lax.axis_index("x")) % 2 == 1


def gather_early(packed, later):
    far_y, far = from_rows(packed, dz=4, dy=1), from_rows(packed, dz=4)
    again, later = lax.optimization_barrier((packed, later))
    four = jnp.stack([packed, from_rows(again, dy=1), far, far_y])
    low = jnp.stack([four, from_axis(four, False, 1)])
    high = jnp.stack([from_axis(four, False, -1), from_axis(four, False, 2)])
    return low, high, later


def gather_near(low, high):
    odd = odd_place()
    forwarded = [from_axis(low, True, 1), from_axis(high, True, -1)]
    low, high = lax.optimization_barrier((low, high))
    others = [exchange(jnp.where(odd, high, low), False), exchange(jnp.where(odd, low, high), True)]
    return forwarded, others


def gather_far(plus, minus):
    return [from_axis(plus, True, 1), from_axis(minus, True, -1)]


def where_held(column):
    owner, block = column // 4, column % 4
    core = lax.axis_index("core")
    dz = (owner // (NY * NX) - lax.axis_index("z")) % NZ
    dy = (owner // NX - lax.axis_index("yh")) % NY
    dx = (owner - lax.axis_index("x")) % NX
    ring = jnp.where(core == 0, dx, dz % 4)
    late = jnp.where(core == 0, dz % 4, dx)
    a = jnp.where(ring == 2, 3, jnp.where(ring == 3, 2, ring))
    upper = (dz >= 3) & (dz <= 6)
    swapped = jnp.where(core == 0, (late == 2) & (a >= 2), (ring == 2) & (lax.axis_index("z") % 2 == 1))
    e = dy + 2 * (upper != swapped).astype(jnp.int32)
    high, odd = a // 2, odd_place().astype(jnp.int32)
    after = jnp.where(high == 0, 2, 4 + odd)
    before = jnp.where(high == 1, 3, 5 - odd)
    source = jnp.where(late == 0, high, jnp.where(late == 1, after, jnp.where(late == 3, before, 6 + high)))
    place = (a % 2 * 4 + e) * 2 + block % 2
    return source, place, block // 2


def tile_table(row, source, place, half, count):
    listed = row.shape[0]
    t = jnp.arange(listed)
    r4, sources = jnp.arange(4), jnp.arange(count)
    key = source * 4 + row
    rank = jnp.sum(((key[None, :] == key[:, None]) & (t[None, :] < t[:, None])).astype(jnp.int32), axis=1)
    held = jnp.sum((key[:, None] == jnp.arange(count * 4)[None, :]).astype(jnp.int32), axis=0).reshape(count, 4)
    need = jnp.max((held + GROUP - 1) // GROUP, axis=1)
    bounds = jnp.sum(jnp.where(sources[None, :] < jnp.arange(count + 1)[:, None], need[None, :], 0), axis=1)
    begin = jnp.sum(jnp.where(source[:, None] == sources[None, :], bounds[None, :count], 0), axis=1)
    slot = ((begin + rank // GROUP) * 4 + row) * GROUP + rank % GROUP
    value = 1 + t + place * 256 + half * 65536
    j = jnp.arange((listed // GROUP + count) * 4 * GROUP)
    table = jnp.sum(jnp.where(slot[None, :] == j[:, None], value[None, :], 0), axis=1)
    return jnp.where(table > 0, table - 1, 2 * 65536).astype(jnp.int32), bounds.astype(jnp.int32)


def add_tiles(table, first, last, adj, blocks, acc, masks):
    def step(s, carry):
        for r in range(4):
            lhs, rhs = [], []
            for u in range(GROUP):
                e = table[(s * 4 + r) * GROUP + u]
                lhs.append(adj[e & 255])
                rhs.append(blocks[(e >> 8) & 255] * masks[e >> 16])
            acc[r] += jnp.dot(
                jnp.concatenate(lhs, axis=1), jnp.concatenate(rhs, axis=0), preferred_element_type=jnp.float32
            )
        return carry

    lax.fori_loop(first, last, step, 0)


def set_masks(masks):
    lane = lax.broadcasted_iota(jnp.int32, (128, 128), 1)
    masks[0] = jnp.where(lane < 64, 1.0, 0.0).astype(masks.dtype)
    masks[1] = jnp.where(lane < 64, 0.0, 1.0).astype(masks.dtype)
    masks[2] = jnp.zeros((128, 128), masks.dtype)
    return lane


def pre_kernel(grad_out, relu_mask, out):
    g = grad_out[...].astype(jnp.float32) * relu_mask[...].astype(jnp.float32)
    out[...] = jnp.concatenate([g[:, :256], g[:, 256:]], axis=0).T.astype(out.dtype)


def masked(grad_out, relu_mask):
    vmem = pl.BlockSpec(memory_space=pltpu.VMEM)
    return pl.pallas_call(
        pre_kernel,
        out_shape=jax.ShapeDtypeStruct((256, 128), jnp.bfloat16),
        in_specs=[vmem, vmem],
        out_specs=vmem,
        name="masked",
    )(grad_out.T, relu_mask.T)


def add_sources(table, bounds, adj, sources, first, acc, masks):
    for k, source in enumerate(sources):
        add_tiles(table, bounds[first + k], bounds[first + k + 1], adj, source, acc, masks)


def first_kernel(table, bounds, adj, *refs):
    *sources, acc, masks = refs
    set_masks(masks)
    acc[...] = jnp.zeros_like(acc)
    add_sources(table, bounds, adj, sources, 0, acc, masks)


def middle_kernel(table, bounds, adj, *refs):
    *sources, before, acc, masks = refs
    set_masks(masks)
    acc[...] = before[...]
    add_sources(table, bounds, adj, sources, 2, acc, masks)


def last_kernel(table, bounds, adj, *refs):
    *sources, before, features, weights, out, out_a, out_b, out_c, partial, acc, masks = refs
    lane = set_masks(masks)
    acc[...] = before[...]
    add_sources(table, bounds, adj, sources, 6, acc, masks)
    agg = [acc[r] + pltpu.roll(acc[r], 64, 1) for r in range(4)]
    rounded = jnp.concatenate([v.astype(jnp.bfloat16) for v in agg], axis=0)
    product = jnp.dot(features[...], rounded, preferred_element_type=jnp.float32)
    low = lax.broadcasted_iota(jnp.int32, (64, 128), 1) < 64
    for p in range(2):
        partial[:, p, :] = jnp.where(low, product[p * 128 : p * 128 + 64], product[p * 128 + 64 : p * 128 + 128])
    for r in range(2):
        packed = jnp.where(lane < 64, agg[r], agg[r + 2]).astype(out.dtype)
        for ref in (out, out_a, out_b, out_c):
            ref[pl.ds(r * 128, 128), :] = packed
    for k, ref in enumerate((out_a, out_b, out_c)):
        ref[pl.ds(256, 64), :] = weights[k]


def call(kernel, table, bounds, adj, sources, others, out_shape, keep_acc, name):
    smem = pl.BlockSpec(memory_space=pltpu.SMEM)
    vmem = pl.BlockSpec(memory_space=pltpu.VMEM)
    sources = [s.reshape(-1, 128, 128) for s in sources]
    return pl.pallas_call(
        kernel,
        out_shape=out_shape,
        in_specs=[smem, smem, vmem] + [vmem] * len(sources) + [vmem] * len(others),
        out_specs=jax.tree.map(lambda _: vmem, out_shape),
        scratch_shapes=([pltpu.VMEM((4, 128, 128), jnp.float32)] if keep_acc else []) + [
            pltpu.VMEM((3, 128, 128), jnp.bfloat16),
        ],
        compiler_params=pltpu.CompilerParams(vmem_limit_bytes=8 * 1024 * 1024),
        cost_estimate=pl.CostEstimate(flops=2 * 64 * 128 * 128 * 128, bytes_accessed=8 * 1024 * 1024, transcendentals=0),
        name=name,
    )(table, bounds, adj, *sources, *others)


def halves(packed):
    return jnp.concatenate([packed[:, :64], packed[:, 64:]], axis=0)


def body(adj_tiles, tile_index, grad_out, relu_mask, features, weight):
    position = lax.axis_index(ROWS)
    slab = lax.axis_index(SLAB)
    source, place, half = where_held(tile_index[:, 1])
    low, high, source = gather_early(masked(grad_out, relu_mask), source)
    forwarded, others = gather_near(low, high)

    tables = tile_table(tile_index[:, 0] - position * 4, source, place, half, 8)
    f_rows = features.reshape(512, 64, 4).transpose(2, 1, 0).reshape(256, 512)
    w_parts = [lax.dynamic_slice_in_dim(weight, (slab ^ k) * 64, 64, 0) for k in range(4)]
    w_sent = jnp.pad(jnp.stack(w_parts[1:]), ((0, 0), (0, 0), (0, 64)))

    sums = jax.ShapeDtypeStruct((4, 128, 128), jnp.float32)
    acc = call(first_kernel, *tables, adj_tiles, [low, high], [], sums, False, "early_tiles")
    forwarded, acc, f_rows, w_sent = lax.optimization_barrier((forwarded, acc, f_rows, w_sent))
    far = gather_far(*forwarded)
    acc = call(middle_kernel, *tables, adj_tiles, forwarded + others, [acc], sums, False, "near_tiles")
    message = jax.ShapeDtypeStruct((320, 128), jnp.bfloat16)
    outs = (jax.ShapeDtypeStruct((256, 128), jnp.bfloat16), message, message, message, jax.ShapeDtypeStruct((64, 2, 128), jnp.float32))
    agg, *messages, partial = call(last_kernel, *tables, adj_tiles, far, [acc, f_rows, w_sent], outs, True, "far_tiles")

    pieces = lax.all_to_all(partial, ROWS, 0, 0, tiled=True)
    arrived = [lax.ppermute(m, SLAB, pairs) for m, pairs in zip(messages, FLIPS)]
    a_all = jnp.concatenate([halves(agg)] + [halves(m[:256]) for m in arrived], axis=1)
    w_all = jnp.concatenate([w_parts[0]] + [m[256:, :64] for m in arrived], axis=1)
    grad_input = jnp.einsum("rs,is->ri", a_all, w_all, preferred_element_type=jnp.float32).astype(jnp.bfloat16)
    total = jnp.sum(pieces, axis=0)
    grad_weight = jnp.concatenate([total[p : p + 1, k : k + 64] for p in range(2) for k in (0, 64)], axis=0)
    return grad_input, grad_weight


def solution(mesh):
    fine = Mesh(mesh.devices.reshape(NZ, NY, NX, NL, NC), ALL)
    return jax.shard_map(
        body,
        mesh=fine,
        in_specs=(P(ROWS, None, None), P(ROWS, None), P(ROWS, SLAB), P(ROWS, SLAB), P(ROWS, None), P(None, SLAB)),
        out_specs=(P(ROWS, SLAB), P(ROWS, SLAB)),
        check_vma=False,
    )
```

```python
import jax
import jax.numpy as jnp
from jax import lax
from jax.experimental import pallas as pl
from jax.experimental.pallas import tpu as pltpu
from jax.sharding import Mesh, PartitionSpec as P

NZ, NY, NX, NL, NC = 8, 2, 4, 2, 2
ROWS = ("z", "yh", "x")
SLAB = ("yl", "core")
ALL = ROWS + SLAB
GROUP = 4
GROUPS = 4
FLIPS = ([(0, 1), (1, 0), (2, 3), (3, 2)], [(0, 2), (2, 0), (1, 3), (3, 1)], [(0, 3), (3, 0), (1, 2), (2, 1)])


def device(z, y, x, l, c):
    return ((((z % NZ) * NY + y % NY) * NX + x % NX) * NL + l) * NC + c


def places():
    return [(z, y, x, l, c) for z in range(NZ) for y in range(NY) for x in range(NX) for l in range(NL) for c in range(NC)]


def from_rows(value, dz=0, dy=0):
    pairs = [(device(z + dz, y + dy, x, l, c), device(z, y, x, l, c)) for z, y, x, l, c in places()]
    return lax.ppermute(value, ALL, pairs)


def from_axis(value, second, step):
    pairs = []
    for z, y, x, l, c in places():
        along_x = (c == 0) != second
        z_step = -step if step == 2 and z % 2 else step
        source = device(z, y, x + step, l, c) if along_x else device(z + z_step, y, x, l, c)
        pairs.append((source, device(z, y, x, l, c)))
    return lax.ppermute(value, ALL, pairs)


def exchange(value, second_pairs):
    pairs = []
    for z, y, x, l, c in places():
        at = z if c == 0 else x
        step = 1 if (at % 2 == 0) != second_pairs else -1
        source = device(z + step, y, x, l, c) if c == 0 else device(z, y, x + step, l, c)
        pairs.append((source, device(z, y, x, l, c)))
    return lax.ppermute(value, ALL, pairs)


def odd_place():
    return jnp.where(lax.axis_index("core") == 0, lax.axis_index("z"), lax.axis_index("x")) % 2 == 1


def gather_early(packed, position):
    far_y, far = from_rows(packed, dz=4, dy=1), from_rows(packed, dz=4)
    again, position = lax.optimization_barrier((packed, position))
    four = jnp.stack([packed, from_rows(again, dy=1), far, far_y])
    low = jnp.stack([four, from_axis(four, False, 1)])
    high = jnp.stack([from_axis(four, False, -1), from_axis(four, False, 2)])
    return low, high, position


def gather_near(low, high):
    odd = odd_place()
    forwarded = [from_axis(low, True, 1), from_axis(high, True, -1)]
    low, high = lax.optimization_barrier((low, high))
    others = [exchange(jnp.where(odd, high, low), False), exchange(jnp.where(odd, low, high), True)]
    return forwarded, others


def gather_far(plus, minus):
    return [from_axis(plus, True, 1), from_axis(minus, True, -1)]


def where_held(column):
    owner, block = column // 4, column % 4
    core = lax.axis_index("core")
    dz = (owner // (NY * NX) - lax.axis_index("z")) % NZ
    dy = (owner // NX - lax.axis_index("yh")) % NY
    dx = (owner - lax.axis_index("x")) % NX
    ring = jnp.where(core == 0, dx, dz % 4)
    late = jnp.where(core == 0, dz % 4, dx)
    a = jnp.where(ring == 2, 3, jnp.where(ring == 3, 2, ring))
    upper = (dz >= 3) & (dz <= 6)
    swapped = jnp.where(core == 0, (late == 2) & (a >= 2), (ring == 2) & (lax.axis_index("z") % 2 == 1))
    e = dy + 2 * (upper != swapped).astype(jnp.int32)
    high, odd = a // 2, odd_place().astype(jnp.int32)
    after = jnp.where(high == 0, 2, 4 + odd)
    before = jnp.where(high == 1, 3, 5 - odd)
    source = jnp.where(late == 0, high, jnp.where(late == 1, after, jnp.where(late == 3, before, 6 + high)))
    place = (a % 2 * 4 + e) * 2 + block % 2
    return source, place, block // 2


def tile_table(row, source, place, half, count):
    listed = row.shape[0]
    t = jnp.arange(listed)
    keys, sources = jnp.arange(count * 4), jnp.arange(count)
    key = source * 4 + row
    rank = jnp.sum(((key[None, :] == key[:, None]) & (t[None, :] < t[:, None])).astype(jnp.int32), axis=1)
    held = jnp.sum((key[:, None] == keys[None, :]).astype(jnp.int32), axis=0)
    need = (held + GROUP - 1) // GROUP
    total = jnp.sum(jnp.where(keys[None, :] // 4 == sources[:, None], need[None, :], 0), axis=1)
    turns = (total + GROUPS - 1) // GROUPS
    bounds = jnp.sum(jnp.where(sources[None, :] < jnp.arange(count + 1)[:, None], turns[None, :], 0), axis=1)
    ahead = (keys[None, :] // 4 == keys[:, None] // 4) & (keys[None, :] < keys[:, None])
    begin = jnp.sum(jnp.where(ahead, need[None, :], 0), axis=1)
    begin = begin + GROUPS * jnp.sum(jnp.where(keys[:, None] // 4 == sources[None, :], bounds[None, :count], 0), axis=1)
    group = jnp.sum(jnp.where(key[:, None] == keys[None, :], begin[None, :], 0), axis=1) + rank // GROUP
    slot = group * GROUP + rank % GROUP
    value = 1 + t + place * 256 + half * 65536 + row * 262144
    most = listed // (GROUP * GROUPS) + (3 * count + 1) // 2
    j = jnp.arange(most * GROUPS * GROUP)
    table = jnp.sum(jnp.where(slot[None, :] == j[:, None], value[None, :], 0), axis=1)
    return jnp.where(table > 0, table - 1, 2 * 65536).astype(jnp.int32), bounds.astype(jnp.int32)


def add_tiles(table, first, last, adj, blocks, acc, masks):
    def step(s, carry):
        products = []
        for g in range(GROUPS):
            lhs, rhs = [], []
            for u in range(GROUP):
                e = table[(s * GROUPS + g) * GROUP + u]
                lhs.append(adj[e & 255])
                block = blocks[(e >> 8) & 255].reshape(8, 16, 128) * masks[(e >> 16) & 3][None]
                rhs.append(block.reshape(128, 128))
            products.append(
                jnp.dot(jnp.concatenate(lhs, axis=1), jnp.concatenate(rhs, axis=0), preferred_element_type=jnp.float32)
            )
        for g, product in enumerate(products):
            acc[table[(s * GROUPS + g) * GROUP] >> 18] += product
        return carry

    lax.fori_loop(first, last, step, 0)


def set_masks(masks):
    lane = lax.broadcasted_iota(jnp.int32, (16, 128), 1)
    masks[0] = jnp.where(lane < 64, 1.0, 0.0).astype(masks.dtype)
    masks[1] = jnp.where(lane < 64, 0.0, 1.0).astype(masks.dtype)
    masks[2] = jnp.zeros((16, 128), masks.dtype)
    return lax.broadcasted_iota(jnp.int32, (128, 128), 1)


def pre_kernel(grad_out, relu_mask, out):
    g = grad_out[...].astype(jnp.float32) * relu_mask[...].astype(jnp.float32)
    out[...] = jnp.concatenate([g[:, :256], g[:, 256:]], axis=0).T.astype(out.dtype)


def masked(grad_out, relu_mask):
    vmem = pl.BlockSpec(memory_space=pltpu.VMEM)
    return pl.pallas_call(
        pre_kernel,
        out_shape=jax.ShapeDtypeStruct((256, 128), jnp.bfloat16),
        in_specs=[vmem, vmem],
        out_specs=vmem,
        name="masked",
    )(grad_out.T, relu_mask.T)


def add_sources(table, bounds, adj, sources, first, acc, masks):
    for k, source in enumerate(sources):
        add_tiles(table, bounds[first + k], bounds[first + k + 1], adj, source, acc, masks)


def first_kernel(table, bounds, adj, *refs):
    *sources, acc, masks = refs
    set_masks(masks)
    acc[...] = jnp.zeros_like(acc)
    add_sources(table, bounds, adj, sources, 0, acc, masks)


def middle_kernel(table, bounds, adj, *refs):
    *sources, before, acc, masks = refs
    set_masks(masks)
    acc[...] = before[...]
    add_sources(table, bounds, adj, sources, 2, acc, masks)


def last_kernel(table, bounds, adj, *refs):
    *sources, before, features, weights, out, out_a, out_b, out_c, partial, acc, masks = refs
    outs = (out, out_a, out_b, out_c)
    lane = set_masks(masks)
    acc[...] = before[...]
    add_sources(table, bounds, adj, sources, 6, acc, masks)
    agg = [acc[r] + pltpu.roll(acc[r], 64, 1) for r in range(4)]
    rounded = jnp.concatenate([v.astype(jnp.bfloat16) for v in agg], axis=0)
    product = jnp.dot(features[...], rounded, preferred_element_type=jnp.float32)
    low = lax.broadcasted_iota(jnp.int32, (64, 128), 1) < 64
    for p in range(2):
        partial[:, p, :] = jnp.where(low, product[p * 128 : p * 128 + 64], product[p * 128 + 64 : p * 128 + 128])
    for r in range(2):
        packed = jnp.where(lane < 64, agg[r], agg[r + 2]).astype(out.dtype)
        for ref in outs:
            ref[pl.ds(r * 128, 128), :] = packed
    for k, ref in enumerate(outs):
        ref[pl.ds(256, 64), :] = weights[:, pl.ds(pl.multiple_of((lax.axis_index("yl") ^ (k >> 1)) * 128, 128), 128)]


def call(kernel, table, bounds, adj, sources, others, out_shape, keep_acc, name):
    smem = pl.BlockSpec(memory_space=pltpu.SMEM)
    vmem = pl.BlockSpec(memory_space=pltpu.VMEM)
    sources = [s.reshape(-1, 128, 128) for s in sources]
    return pl.pallas_call(
        kernel,
        out_shape=out_shape,
        in_specs=[smem, smem, vmem] + [vmem] * len(sources) + [vmem] * len(others),
        out_specs=jax.tree.map(lambda _: vmem, out_shape),
        scratch_shapes=([pltpu.VMEM((4, 128, 128), jnp.float32)] if keep_acc else []) + [
            pltpu.VMEM((3, 16, 128), jnp.bfloat16),
        ],
        compiler_params=pltpu.CompilerParams(vmem_limit_bytes=4 * 1024 * 1024),
        cost_estimate=pl.CostEstimate(flops=2 * 64 * 128 * 128 * 128, bytes_accessed=8 * 1024 * 1024, transcendentals=0),
        name=name,
    )(table, bounds, adj, *sources, *others)


def halves(packed):
    return jnp.concatenate([packed[:, :64], packed[:, 64:]], axis=0)


def body(adj_tiles, tile_index, grad_out, relu_mask, features, weight):
    position = lax.axis_index(ROWS)
    source, place, half = where_held(tile_index[:, 1])
    low, high, position = gather_early(masked(grad_out, relu_mask), position)
    forwarded, others = gather_near(low, high)

    tables = tile_table(tile_index[:, 0] - position * 4, source, place, half, 8)
    f_rows = features.reshape(512, 64, 4).transpose(2, 1, 0).reshape(256, 512)
    low, high, tables, f_rows = lax.optimization_barrier((low, high, tables, f_rows))

    sums = jax.ShapeDtypeStruct((4, 128, 128), jnp.float32)
    acc = call(first_kernel, *tables, adj_tiles, [low, high], [], sums, False, "early_tiles")
    forwarded, acc = lax.optimization_barrier((forwarded, acc))
    far = gather_far(*forwarded)
    acc = call(middle_kernel, *tables, adj_tiles, forwarded + others, [acc], sums, False, "near_tiles")
    message = jax.ShapeDtypeStruct((320, 128), jnp.bfloat16)
    outs = (message, message, message, message, jax.ShapeDtypeStruct((64, 2, 128), jnp.float32))
    *messages, partial = call(last_kernel, *tables, adj_tiles, far, [acc, f_rows, weight.T], outs, True, "far_tiles")

    pieces = lax.all_to_all(partial, ROWS, 0, 0, tiled=True)
    arrived = messages[:1] + [lax.ppermute(m, SLAB, pairs) for m, pairs in zip(messages[1:], FLIPS)]
    a_all = jnp.concatenate([halves(m[:256]) for m in arrived], axis=1)
    w_all = jnp.concatenate([m[256:] for m in arrived], axis=0)
    w_all = jnp.where(lax.axis_index("core") == 0, w_all[:, :64], w_all[:, 64:])
    grad_input = jnp.einsum("rs,si->ri", a_all, w_all, preferred_element_type=jnp.float32).astype(jnp.bfloat16)
    total = jnp.sum(pieces, axis=0)
    grad_weight = jnp.concatenate([total[p : p + 1, k : k + 64] for p in range(2) for k in (0, 64)], axis=0)
    return grad_input, grad_weight


def solution(mesh):
    fine = Mesh(mesh.devices.reshape(NZ, NY, NX, NL, NC), ALL)
    return jax.shard_map(
        body,
        mesh=fine,
        in_specs=(P(ROWS, None, None), P(ROWS, None), P(ROWS, SLAB), P(ROWS, SLAB), P(ROWS, None), P(None, SLAB)),
        out_specs=(P(ROWS, SLAB), P(ROWS, SLAB)),
        check_vma=False,
    )
```

```python
import jax
import jax.numpy as jnp
from jax import lax
from jax.experimental import pallas as pl
from jax.experimental.pallas import tpu as pltpu
from jax.sharding import Mesh, PartitionSpec as P

NZ, NY, NX, NL, NC = 8, 2, 4, 2, 2
ROWS = ("z", "yh", "x")
SLAB = ("yl", "core")
ALL = ROWS + SLAB
GROUP = 4
GROUPS = 4
OTHER = [(0, 1), (1, 0)]


def device(z, y, x, l, c):
    return ((((z % NZ) * NY + y % NY) * NX + x % NX) * NL + l) * NC + c


def places():
    return [(z, y, x, l, c) for z in range(NZ) for y in range(NY) for x in range(NX) for l in range(NL) for c in range(NC)]


def from_rows(value, dz=0, dy=0):
    pairs = [(device(z + dz, y + dy, x, l, c), device(z, y, x, l, c)) for z, y, x, l, c in places()]
    return lax.ppermute(value, ALL, pairs)


def from_axis(value, second, step):
    pairs = []
    for z, y, x, l, c in places():
        along_x = (c == 0) != second
        z_step = -step if step == 2 and z % 2 else step
        source = device(z, y, x + step, l, c) if along_x else device(z + z_step, y, x, l, c)
        pairs.append((source, device(z, y, x, l, c)))
    return lax.ppermute(value, ALL, pairs)


def exchange(value, second_pairs):
    pairs = []
    for z, y, x, l, c in places():
        at = z if c == 0 else x
        step = 1 if (at % 2 == 0) != second_pairs else -1
        source = device(z + step, y, x, l, c) if c == 0 else device(z, y, x + step, l, c)
        pairs.append((source, device(z, y, x, l, c)))
    return lax.ppermute(value, ALL, pairs)


def odd_place():
    return jnp.where(lax.axis_index("core") == 0, lax.axis_index("z"), lax.axis_index("x")) % 2 == 1


def gather_early(packed, position):
    far, far_y = from_rows(packed, dz=4), from_rows(packed, dz=4, dy=1)
    again, position = lax.optimization_barrier((packed, position))
    near_y = from_rows(again, dy=1)
    pairs = [jnp.stack([packed, far]), jnp.stack([near_y, far_y])]
    one, back, two = [[from_axis(pair, False, step) for pair in pairs] for step in (1, -1, 2)]
    low = jnp.stack(pairs + one).reshape(2, 4, 256, 128)
    high = jnp.stack(back + two).reshape(2, 4, 256, 128)
    return low, high, position


def gather_near(low, high):
    odd = odd_place()
    forwarded = [from_axis(low, True, 1), from_axis(high, True, -1)]
    low, high = lax.optimization_barrier((low, high))
    others = [exchange(jnp.where(odd, high, low), False), exchange(jnp.where(odd, low, high), True)]
    return forwarded, others


def gather_far(plus, minus):
    return [from_axis(plus, True, 1), from_axis(minus, True, -1)]


def where_held(column):
    owner, block = column // 4, column % 4
    core = lax.axis_index("core")
    dz = (owner // (NY * NX) - lax.axis_index("z")) % NZ
    dy = (owner // NX - lax.axis_index("yh")) % NY
    dx = (owner - lax.axis_index("x")) % NX
    ring = jnp.where(core == 0, dx, dz % 4)
    late = jnp.where(core == 0, dz % 4, dx)
    a = jnp.where(ring == 2, 3, jnp.where(ring == 3, 2, ring))
    upper = (dz >= 3) & (dz <= 6)
    swapped = jnp.where(core == 0, (late == 2) & (a >= 2), (ring == 2) & (lax.axis_index("z") % 2 == 1))
    e = 2 * dy + (upper != swapped).astype(jnp.int32)
    high, odd = a // 2, odd_place().astype(jnp.int32)
    after = jnp.where(high == 0, 2, 4 + odd)
    before = jnp.where(high == 1, 3, 5 - odd)
    source = jnp.where(late == 0, high, jnp.where(late == 1, after, jnp.where(late == 3, before, 6 + high)))
    place = (a % 2 * 4 + e) * 2 + block % 2
    return source, place, block // 2


def tile_table(row, source, place, half, count):
    listed = row.shape[0]
    t = jnp.arange(listed)
    keys, sources = jnp.arange(count * 4), jnp.arange(count)
    key = source * 4 + row
    rank = jnp.sum(((key[None, :] == key[:, None]) & (t[None, :] < t[:, None])).astype(jnp.int32), axis=1)
    held = jnp.sum((key[:, None] == keys[None, :]).astype(jnp.int32), axis=0)
    need = (held + GROUP - 1) // GROUP
    total = jnp.sum(jnp.where(keys[None, :] // 4 == sources[:, None], need[None, :], 0), axis=1)
    turns = (total + GROUPS - 1) // GROUPS
    bounds = jnp.sum(jnp.where(sources[None, :] < jnp.arange(count + 1)[:, None], turns[None, :], 0), axis=1)
    ahead = (keys[None, :] // 4 == keys[:, None] // 4) & (keys[None, :] < keys[:, None])
    begin = jnp.sum(jnp.where(ahead, need[None, :], 0), axis=1)
    begin = begin + GROUPS * jnp.sum(jnp.where(keys[:, None] // 4 == sources[None, :], bounds[None, :count], 0), axis=1)
    group = jnp.sum(jnp.where(key[:, None] == keys[None, :], begin[None, :], 0), axis=1) + rank // GROUP
    slot = group * GROUP + rank % GROUP
    value = 1 + t + place * 256 + half * 65536 + row * 262144
    most = listed // (GROUP * GROUPS) + (3 * count + 1) // 2
    j = jnp.arange(most * GROUPS * GROUP)
    table = jnp.sum(jnp.where(slot[None, :] == j[:, None], value[None, :], 0), axis=1)
    return jnp.where(table > 0, table - 1, 2 * 65536).astype(jnp.int32), bounds.astype(jnp.int32)


def add_tiles(table, first, last, adj, blocks, acc, masks):
    def step(s, carry):
        products = []
        for g in range(GROUPS):
            lhs, rhs = [], []
            for u in range(GROUP):
                e = table[(s * GROUPS + g) * GROUP + u]
                lhs.append(adj[e & 255])
                block = blocks[(e >> 8) & 255].reshape(8, 16, 128) * masks[(e >> 16) & 3][None]
                rhs.append(block.reshape(128, 128))
            products.append(
                jnp.dot(jnp.concatenate(lhs, axis=1), jnp.concatenate(rhs, axis=0), preferred_element_type=jnp.float32)
            )
        for g, product in enumerate(products):
            acc[table[(s * GROUPS + g) * GROUP] >> 18] += product
        return carry

    lax.fori_loop(first, last, step, 0)


def set_masks(masks):
    lane = lax.broadcasted_iota(jnp.int32, (16, 128), 1)
    masks[0] = jnp.where(lane < 64, 1.0, 0.0).astype(masks.dtype)
    masks[1] = jnp.where(lane < 64, 0.0, 1.0).astype(masks.dtype)
    masks[2] = jnp.zeros((16, 128), masks.dtype)
    return lax.broadcasted_iota(jnp.int32, (128, 128), 1)


def pre_kernel(grad_out, relu_mask, out):
    g = grad_out[...].astype(jnp.float32) * relu_mask[...].astype(jnp.float32)
    out[...] = jnp.concatenate([g[:, :256], g[:, 256:]], axis=0).T.astype(out.dtype)


def masked(grad_out, relu_mask):
    vmem = pl.BlockSpec(memory_space=pltpu.VMEM)
    return pl.pallas_call(
        pre_kernel,
        out_shape=jax.ShapeDtypeStruct((256, 128), jnp.bfloat16),
        in_specs=[vmem, vmem],
        out_specs=vmem,
        name="masked",
    )(grad_out.T, relu_mask.T)


def add_sources(table, bounds, adj, sources, first, acc, masks):
    for k, source in enumerate(sources):
        add_tiles(table, bounds[first + k], bounds[first + k + 1], adj, source, acc, masks)


def first_kernel(table, bounds, adj, *refs):
    *sources, acc, masks = refs
    set_masks(masks)
    acc[...] = jnp.zeros_like(acc)
    add_sources(table, bounds, adj, sources, 0, acc, masks)


def middle_kernel(table, bounds, adj, *refs):
    *sources, before, acc, masks = refs
    set_masks(masks)
    acc[...] = before[...]
    add_sources(table, bounds, adj, sources, 2, acc, masks)


def last_kernel(table, bounds, adj, *refs):
    *sources, before, features, weights, out, partial, acc, masks = refs
    lane = set_masks(masks)
    acc[...] = before[...]
    add_sources(table, bounds, adj, sources, 6, acc, masks)
    agg = [acc[r] + pltpu.roll(acc[r], 64, 1) for r in range(4)]
    rounded = jnp.concatenate([v.astype(jnp.bfloat16) for v in agg], axis=0)
    product = jnp.dot(features[...], rounded, preferred_element_type=jnp.float32)
    low = lax.broadcasted_iota(jnp.int32, (64, 128), 1) < 64
    for p in range(2):
        partial[:, p, :] = jnp.where(low, product[p * 128 : p * 128 + 64], product[p * 128 + 64 : p * 128 + 128])
    for r in range(2):
        out[pl.ds(r * 128, 128), :] = jnp.where(lane < 64, agg[r], agg[r + 2]).astype(out.dtype)
    for k in range(2):
        lanes = pl.multiple_of((lax.axis_index("yl") ^ (1 - k)) * 128, 128)
        out[pl.ds(256 + k * 64, 64), :] = weights[:, pl.ds(lanes, 128)]


def call(kernel, table, bounds, adj, sources, others, out_shape, keep_acc, name):
    smem = pl.BlockSpec(memory_space=pltpu.SMEM)
    vmem = pl.BlockSpec(memory_space=pltpu.VMEM)
    sources = [s.reshape(-1, 128, 128) for s in sources]
    return pl.pallas_call(
        kernel,
        out_shape=out_shape,
        in_specs=[smem, smem, vmem] + [vmem] * len(sources) + [vmem] * len(others),
        out_specs=jax.tree.map(lambda _: vmem, out_shape),
        scratch_shapes=([pltpu.VMEM((4, 128, 128), jnp.float32)] if keep_acc else []) + [
            pltpu.VMEM((3, 16, 128), jnp.bfloat16),
        ],
        compiler_params=pltpu.CompilerParams(vmem_limit_bytes=4 * 1024 * 1024),
        cost_estimate=pl.CostEstimate(flops=2 * 64 * 128 * 128 * 128, bytes_accessed=8 * 1024 * 1024, transcendentals=0),
        name=name,
    )(table, bounds, adj, *sources, *others)


def halves(packed):
    return jnp.concatenate([packed[:, :64], packed[:, 64:]], axis=0)


def body(adj_tiles, tile_index, grad_out, relu_mask, features, weight):
    position = lax.axis_index(ROWS)
    source, place, half = where_held(tile_index[:, 1])
    low, high, position = gather_early(masked(grad_out, relu_mask), position)
    forwarded, others = gather_near(low, high)

    tables = tile_table(tile_index[:, 0] - position * 4, source, place, half, 8)
    f_rows = features.reshape(512, 64, 4).transpose(2, 1, 0).reshape(256, 512)
    low, high, tables, f_rows = lax.optimization_barrier((low, high, tables, f_rows))

    sums = jax.ShapeDtypeStruct((4, 128, 128), jnp.float32)
    acc = call(first_kernel, *tables, adj_tiles, [low, high], [], sums, False, "early_tiles")
    forwarded, acc = lax.optimization_barrier((forwarded, acc))
    far = gather_far(*forwarded)
    acc = call(middle_kernel, *tables, adj_tiles, forwarded + others, [acc], sums, False, "near_tiles")
    outs = (jax.ShapeDtypeStruct((384, 128), jnp.bfloat16), jax.ShapeDtypeStruct((64, 2, 128), jnp.float32))
    own, partial = call(last_kernel, *tables, adj_tiles, far, [acc, f_rows, weight.T], outs, True, "far_tiles")

    other_core = lax.ppermute(own, "core", OTHER)
    pieces = lax.all_to_all(partial, ROWS, 0, 0, tiled=True)
    other_chip = lax.ppermute(jnp.stack([own[:320], other_core[:320]]), "yl", OTHER)
    arrived = [own, other_core, other_chip[0], other_chip[1]]
    a_all = jnp.concatenate([halves(m[:256]) for m in arrived], axis=1)
    w_all = jnp.concatenate([own[320:], other_core[320:], other_chip[0, 256:], other_chip[1, 256:]], axis=0)
    w_all = jnp.where(lax.axis_index("core") == 0, w_all[:, :64], w_all[:, 64:])
    grad_input = jnp.einsum("rs,si->ri", a_all, w_all, preferred_element_type=jnp.float32).astype(jnp.bfloat16)
    total = jnp.sum(pieces, axis=0)
    grad_weight = jnp.concatenate([total[p : p + 1, k : k + 64] for p in range(2) for k in (0, 64)], axis=0)
    return grad_input, grad_weight


def solution(mesh):
    fine = Mesh(mesh.devices.reshape(NZ, NY, NX, NL, NC), ALL)
    return jax.shard_map(
        body,
        mesh=fine,
        in_specs=(P(ROWS, None, None), P(ROWS, None), P(ROWS, SLAB), P(ROWS, SLAB), P(ROWS, None), P(None, SLAB)),
        out_specs=(P(ROWS, SLAB), P(ROWS, SLAB)),
        check_vma=False,
    )
```

```python
import jax
import jax.numpy as jnp
from jax import lax
from jax.experimental import pallas as pl
from jax.experimental.pallas import tpu as pltpu
from jax.sharding import Mesh, PartitionSpec as P

NZ, NY, NX, NL, NC = 8, 2, 4, 2, 2
ROWS = ("z", "yh", "x")
SLAB = ("yl", "core")
ALL = ROWS + SLAB
GROUP = 4
GROUPS = 4
FLIPS = ([(0, 1), (1, 0), (2, 3), (3, 2)], [(0, 2), (2, 0), (1, 3), (3, 1)], [(0, 3), (3, 0), (1, 2), (2, 1)])


def device(z, y, x, l, c):
    return ((((z % NZ) * NY + y % NY) * NX + x % NX) * NL + l) * NC + c


def places():
    return [(z, y, x, l, c) for z in range(NZ) for y in range(NY) for x in range(NX) for l in range(NL) for c in range(NC)]


def from_rows(value, dz=0, dy=0):
    pairs = [(device(z + dz, y + dy, x, l, c), device(z, y, x, l, c)) for z, y, x, l, c in places()]
    return lax.ppermute(value, ALL, pairs)


def from_axis(value, second, step):
    pairs = []
    for z, y, x, l, c in places():
        along_x = (c == 0) != second
        z_step = -step if step == 2 and z % 2 else step
        source = device(z, y, x + step, l, c) if along_x else device(z + z_step, y, x, l, c)
        pairs.append((source, device(z, y, x, l, c)))
    return lax.ppermute(value, ALL, pairs)


def exchange(value, second_pairs):
    pairs = []
    for z, y, x, l, c in places():
        at = z if c == 0 else x
        step = 1 if (at % 2 == 0) != second_pairs else -1
        source = device(z + step, y, x, l, c) if c == 0 else device(z, y, x + step, l, c)
        pairs.append((source, device(z, y, x, l, c)))
    return lax.ppermute(value, ALL, pairs)


def odd_place():
    return jnp.where(lax.axis_index("core") == 0, lax.axis_index("z"), lax.axis_index("x")) % 2 == 1


def gather_early(packed, position):
    far_y, far = from_rows(packed, dz=4, dy=1), from_rows(packed, dz=4)
    again, position = lax.optimization_barrier((packed, position))
    four = jnp.stack([packed, from_rows(again, dy=1), far, far_y])
    low = jnp.stack([lax.optimization_barrier(four), from_axis(four, False, 1)])
    high = jnp.stack([from_axis(four, False, -1), from_axis(four, False, 2)])
    return low, high, position


def gather_near(low, high):
    odd = odd_place()
    forwarded = [from_axis(low, True, 1), from_axis(high, True, -1)]
    low, high = lax.optimization_barrier((low, high))
    others = [exchange(jnp.where(odd, high, low), False), exchange(jnp.where(odd, low, high), True)]
    return forwarded, others


def gather_far(plus, minus):
    return [from_axis(plus, True, 1), from_axis(minus, True, -1)]


def where_held(column):
    owner, block = column // 4, column % 4
    core = lax.axis_index("core")
    dz = (owner // (NY * NX) - lax.axis_index("z")) % NZ
    dy = (owner // NX - lax.axis_index("yh")) % NY
    dx = (owner - lax.axis_index("x")) % NX
    ring = jnp.where(core == 0, dx, dz % 4)
    late = jnp.where(core == 0, dz % 4, dx)
    a = jnp.where(ring == 2, 3, jnp.where(ring == 3, 2, ring))
    upper = (dz >= 3) & (dz <= 6)
    swapped = jnp.where(core == 0, (late == 2) & (a >= 2), (ring == 2) & (lax.axis_index("z") % 2 == 1))
    e = dy + 2 * (upper != swapped).astype(jnp.int32)
    high, odd = a // 2, odd_place().astype(jnp.int32)
    after = jnp.where(high == 0, 2, 4 + odd)
    before = jnp.where(high == 1, 3, 5 - odd)
    source = jnp.where(late == 0, high, jnp.where(late == 1, after, jnp.where(late == 3, before, 6 + high)))
    place = (a % 2 * 4 + e) * 2 + block % 2
    return source, place, block // 2


def tile_table(row, source, place, half, count):
    listed = row.shape[0]
    t = jnp.arange(listed)
    keys, sources = jnp.arange(count * 4), jnp.arange(count)
    key = source * 4 + row
    rank = jnp.sum(((key[None, :] == key[:, None]) & (t[None, :] < t[:, None])).astype(jnp.int32), axis=1)
    held = jnp.sum((key[:, None] == keys[None, :]).astype(jnp.int32), axis=0)
    need = (held + GROUP - 1) // GROUP
    total = jnp.sum(jnp.where(keys[None, :] // 4 == sources[:, None], need[None, :], 0), axis=1)
    turns = (total + GROUPS - 1) // GROUPS
    bounds = jnp.sum(jnp.where(sources[None, :] < jnp.arange(count + 1)[:, None], turns[None, :], 0), axis=1)
    ahead = (keys[None, :] // 4 == keys[:, None] // 4) & (keys[None, :] < keys[:, None])
    begin = jnp.sum(jnp.where(ahead, need[None, :], 0), axis=1)
    begin = begin + GROUPS * jnp.sum(jnp.where(keys[:, None] // 4 == sources[None, :], bounds[None, :count], 0), axis=1)
    group = jnp.sum(jnp.where(key[:, None] == keys[None, :], begin[None, :], 0), axis=1) + rank // GROUP
    slot = group * GROUP + rank % GROUP
    value = 1 + t + place * 256 + half * 65536 + row * 262144
    most = listed // (GROUP * GROUPS) + (3 * count + 1) // 2
    j = jnp.arange(most * GROUPS * GROUP)
    table = jnp.sum(jnp.where(slot[None, :] == j[:, None], value[None, :], 0), axis=1)
    return jnp.where(table > 0, table - 1, 2 * 65536).astype(jnp.int32), bounds.astype(jnp.int32)


def add_tiles(table, first, last, adj, blocks, acc, masks):
    def step(s, carry):
        products = []
        for g in range(GROUPS):
            lhs, rhs = [], []
            for u in range(GROUP):
                e = table[(s * GROUPS + g) * GROUP + u]
                lhs.append(adj[e & 255])
                block = blocks[(e >> 8) & 255].reshape(8, 16, 128) * masks[(e >> 16) & 3][None]
                rhs.append(block.reshape(128, 128))
            products.append(
                jnp.dot(jnp.concatenate(lhs, axis=1), jnp.concatenate(rhs, axis=0), preferred_element_type=jnp.float32)
            )
        for g, product in enumerate(products):
            acc[table[(s * GROUPS + g) * GROUP] >> 18] += product
        return carry

    lax.fori_loop(first, last, step, 0)


def set_masks(masks):
    lane = lax.broadcasted_iota(jnp.int32, (16, 128), 1)
    masks[0] = jnp.where(lane < 64, 1.0, 0.0).astype(masks.dtype)
    masks[1] = jnp.where(lane < 64, 0.0, 1.0).astype(masks.dtype)
    masks[2] = jnp.zeros((16, 128), masks.dtype)
    return lax.broadcasted_iota(jnp.int32, (128, 128), 1)


def pre_kernel(grad_out, relu_mask, out):
    g = grad_out[...].astype(jnp.float32) * relu_mask[...].astype(jnp.float32)
    out[...] = jnp.concatenate([g[:, :256], g[:, 256:]], axis=0).T.astype(out.dtype)


def masked(grad_out, relu_mask):
    vmem = pl.BlockSpec(memory_space=pltpu.VMEM)
    return pl.pallas_call(
        pre_kernel,
        out_shape=jax.ShapeDtypeStruct((256, 128), jnp.bfloat16),
        in_specs=[vmem, vmem],
        out_specs=vmem,
        name="masked",
    )(grad_out.T, relu_mask.T)


def add_sources(table, bounds, adj, sources, first, acc, masks):
    for k, source in enumerate(sources):
        add_tiles(table, bounds[first + k], bounds[first + k + 1], adj, source, acc, masks)


def first_kernel(table, bounds, adj, *refs):
    *sources, acc, masks = refs
    set_masks(masks)
    acc[...] = jnp.zeros_like(acc)
    add_sources(table, bounds, adj, sources, 0, acc, masks)


def middle_kernel(table, bounds, adj, *refs):
    *sources, before, acc, masks = refs
    set_masks(masks)
    acc[...] = before[...]
    add_sources(table, bounds, adj, sources, 2, acc, masks)


def last_kernel(table, bounds, adj, *refs):
    *sources, before, features, weights, out, out_a, out_b, out_c, partial, acc, masks = refs
    outs = (out, out_a, out_b, out_c)
    lane = set_masks(masks)
    acc[...] = before[...]
    add_sources(table, bounds, adj, sources, 6, acc, masks)
    agg = [acc[r] + pltpu.roll(acc[r], 64, 1) for r in range(4)]
    rounded = jnp.concatenate([v.astype(jnp.bfloat16) for v in agg], axis=0)
    product = jnp.dot(features[...], rounded, preferred_element_type=jnp.float32)
    low = lax.broadcasted_iota(jnp.int32, (64, 128), 1) < 64
    for p in range(2):
        partial[:, p, :] = jnp.where(low, product[p * 128 : p * 128 + 64], product[p * 128 + 64 : p * 128 + 128])
    for r in range(2):
        packed = jnp.where(lane < 64, agg[r], agg[r + 2]).astype(out.dtype)
        for ref in outs:
            ref[pl.ds(r * 128, 128), :] = packed
    for k, ref in enumerate(outs):
        lanes = pl.multiple_of((lax.axis_index("yl") ^ (k >> 1)) * 128, 128)
        of_chip = weights[:, pl.ds(lanes, 128)].astype(jnp.float32)
        of_core = jnp.where((lax.axis_index("core") ^ (k & 1)) == 0, of_chip, pltpu.roll(of_chip, 64, 1))
        ref[pl.ds(256, 64), :] = of_core.astype(ref.dtype)


def call(kernel, table, bounds, adj, sources, others, out_shape, keep_acc, name):
    smem = pl.BlockSpec(memory_space=pltpu.SMEM)
    vmem = pl.BlockSpec(memory_space=pltpu.VMEM)
    sources = [s.reshape(-1, 128, 128) for s in sources]
    return pl.pallas_call(
        kernel,
        out_shape=out_shape,
        in_specs=[smem, smem, vmem] + [vmem] * len(sources) + [vmem] * len(others),
        out_specs=jax.tree.map(lambda _: vmem, out_shape),
        scratch_shapes=([pltpu.VMEM((4, 128, 128), jnp.float32)] if keep_acc else []) + [
            pltpu.VMEM((3, 16, 128), jnp.bfloat16),
        ],
        compiler_params=pltpu.CompilerParams(vmem_limit_bytes=4 * 1024 * 1024),
        cost_estimate=pl.CostEstimate(flops=2 * 64 * 128 * 128 * 128, bytes_accessed=8 * 1024 * 1024, transcendentals=0),
        name=name,
    )(table, bounds, adj, *sources, *others)


def halves(packed):
    return jnp.concatenate([packed[:, :64], packed[:, 64:]], axis=0)


def body(adj_tiles, tile_index, grad_out, relu_mask, features, weight):
    position = lax.axis_index(ROWS)
    source, place, half = where_held(tile_index[:, 1])
    low, high, position = gather_early(masked(grad_out, relu_mask), position)
    forwarded, others = gather_near(low, high)

    tables = tile_table(tile_index[:, 0] - position * 4, source, place, half, 8)
    f_rows = features.reshape(512, 64, 4).transpose(2, 1, 0).reshape(256, 512)
    low, high, tables, f_rows = lax.optimization_barrier((low, high, tables, f_rows))

    sums = jax.ShapeDtypeStruct((4, 128, 128), jnp.float32)
    acc = call(first_kernel, *tables, adj_tiles, [low, high], [], sums, False, "early_tiles")
    forwarded, acc = lax.optimization_barrier((forwarded, acc))
    far = gather_far(*forwarded)
    acc = call(middle_kernel, *tables, adj_tiles, forwarded + others, [acc], sums, False, "near_tiles")
    message = jax.ShapeDtypeStruct((320, 128), jnp.bfloat16)
    outs = (message, message, message, message, jax.ShapeDtypeStruct((64, 2, 128), jnp.float32))
    *messages, partial = call(last_kernel, *tables, adj_tiles, far, [acc, f_rows, weight.T], outs, True, "far_tiles")

    pieces = lax.all_to_all(partial, ROWS, 0, 0, tiled=True)
    arrived = messages[:1] + [lax.ppermute(m, SLAB, pairs) for m, pairs in zip(messages[1:], FLIPS)]
    a_all = jnp.concatenate([halves(m[:256]) for m in arrived], axis=1)
    w_all = jnp.concatenate([m[256:, :64] for m in arrived], axis=0)
    grad_input = jnp.einsum("rs,si->ri", a_all, w_all, preferred_element_type=jnp.float32).astype(jnp.bfloat16)
    total = jnp.sum(pieces, axis=0)
    grad_weight = jnp.concatenate([total[p : p + 1, k : k + 64] for p in range(2) for k in (0, 64)], axis=0)
    return grad_input, grad_weight


def solution(mesh):
    fine = Mesh(mesh.devices.reshape(NZ, NY, NX, NL, NC), ALL)
    return jax.shard_map(
        body,
        mesh=fine,
        in_specs=(P(ROWS, None, None), P(ROWS, None), P(ROWS, SLAB), P(ROWS, SLAB), P(ROWS, None), P(None, SLAB)),
        out_specs=(P(ROWS, SLAB), P(ROWS, SLAB)),
        check_vma=False,
    )
```

```python
import jax
import jax.numpy as jnp
from jax import lax
from jax.experimental import pallas as pl
from jax.experimental.pallas import tpu as pltpu
from jax.sharding import Mesh, PartitionSpec as P

NZ, NY, NX, NL, NC = 8, 2, 4, 2, 2
ROWS = ("z", "yh", "x")
SLAB = ("yl", "core")
ALL = ROWS + SLAB
GROUP = 4
GROUPS = 4
FLIPS = ([(0, 1), (1, 0), (2, 3), (3, 2)], [(0, 2), (2, 0), (1, 3), (3, 1)], [(0, 3), (3, 0), (1, 2), (2, 1)])


def device(z, y, x, l, c):
    return ((((z % NZ) * NY + y % NY) * NX + x % NX) * NL + l) * NC + c


def places():
    return [(z, y, x, l, c) for z in range(NZ) for y in range(NY) for x in range(NX) for l in range(NL) for c in range(NC)]


def from_rows(value, dz=0, dy=0):
    pairs = [(device(z + dz, y + dy, x, l, c), device(z, y, x, l, c)) for z, y, x, l, c in places()]
    return lax.ppermute(value, ALL, pairs)


def from_axis(value, second, step):
    pairs = []
    for z, y, x, l, c in places():
        along_x = (c == 0) != second
        z_step = -step if step == 2 and z % 2 else step
        source = device(z, y, x + step, l, c) if along_x else device(z + z_step, y, x, l, c)
        pairs.append((source, device(z, y, x, l, c)))
    return lax.ppermute(value, ALL, pairs)


def exchange(value, second_pairs):
    pairs = []
    for z, y, x, l, c in places():
        at = z if c == 0 else x
        step = 1 if (at % 2 == 0) != second_pairs else -1
        source = device(z + step, y, x, l, c) if c == 0 else device(z, y, x + step, l, c)
        pairs.append((source, device(z, y, x, l, c)))
    return lax.ppermute(value, ALL, pairs)


def odd_place():
    return jnp.where(lax.axis_index("core") == 0, lax.axis_index("z"), lax.axis_index("x")) % 2 == 1


def gather_early(packed, position):
    far_y, far = from_rows(packed, dz=4, dy=1), from_rows(packed, dz=4)
    again, position = lax.optimization_barrier((packed, position))
    four = jnp.stack([packed, from_rows(again, dy=1), far, far_y])
    high = jnp.stack([from_axis(four, False, -1), from_axis(four, False, 2)])
    low = jnp.stack([lax.optimization_barrier(four), from_axis(four, False, 1)])
    return low, high, position


def gather_near(low, high):
    odd = odd_place()
    minus = from_axis(high, True, -1)
    forwarded = [from_axis(low, True, 1), minus]
    low, high = lax.optimization_barrier((low, high))
    others = [exchange(jnp.where(odd, high, low), False), exchange(jnp.where(odd, low, high), True)]
    return forwarded, others


def gather_far(plus, minus):
    return [from_axis(plus, True, 1), from_axis(minus, True, -1)]


def where_held(column):
    owner, block = column // 4, column % 4
    core = lax.axis_index("core")
    dz = (owner // (NY * NX) - lax.axis_index("z")) % NZ
    dy = (owner // NX - lax.axis_index("yh")) % NY
    dx = (owner - lax.axis_index("x")) % NX
    ring = jnp.where(core == 0, dx, dz % 4)
    late = jnp.where(core == 0, dz % 4, dx)
    a = jnp.where(ring == 2, 3, jnp.where(ring == 3, 2, ring))
    upper = (dz >= 3) & (dz <= 6)
    swapped = jnp.where(core == 0, (late == 2) & (a >= 2), (ring == 2) & (lax.axis_index("z") % 2 == 1))
    e = dy + 2 * (upper != swapped).astype(jnp.int32)
    high, odd = a // 2, odd_place().astype(jnp.int32)
    after = jnp.where(high == 0, 2, 4 + odd)
    before = jnp.where(high == 1, 3, 5 - odd)
    source = jnp.where(late == 0, high, jnp.where(late == 1, after, jnp.where(late == 3, before, 6 + high)))
    place = (a % 2 * 4 + e) * 2 + block % 2
    return source, place, block // 2


def tile_table(row, source, place, half, count):
    listed = row.shape[0]
    t = jnp.arange(listed)
    keys, sources = jnp.arange(count * 4), jnp.arange(count)
    key = source * 4 + row
    rank = jnp.sum(((key[None, :] == key[:, None]) & (t[None, :] < t[:, None])).astype(jnp.int32), axis=1)
    held = jnp.sum((key[:, None] == keys[None, :]).astype(jnp.int32), axis=0)
    need = (held + GROUP - 1) // GROUP
    total = jnp.sum(jnp.where(keys[None, :] // 4 == sources[:, None], need[None, :], 0), axis=1)
    turns = (total + GROUPS - 1) // GROUPS
    bounds = jnp.sum(jnp.where(sources[None, :] < jnp.arange(count + 1)[:, None], turns[None, :], 0), axis=1)
    ahead = (keys[None, :] // 4 == keys[:, None] // 4) & (keys[None, :] < keys[:, None])
    begin = jnp.sum(jnp.where(ahead, need[None, :], 0), axis=1)
    begin = begin + GROUPS * jnp.sum(jnp.where(keys[:, None] // 4 == sources[None, :], bounds[None, :count], 0), axis=1)
    group = jnp.sum(jnp.where(key[:, None] == keys[None, :], begin[None, :], 0), axis=1) + rank // GROUP
    slot = group * GROUP + rank % GROUP
    value = 1 + t + place * 256 + half * 65536 + row * 262144
    most = listed // (GROUP * GROUPS) + (3 * count + 1) // 2
    j = jnp.arange(most * GROUPS * GROUP)
    table = jnp.sum(jnp.where(slot[None, :] == j[:, None], value[None, :], 0), axis=1)
    return jnp.where(table > 0, table - 1, 2 * 65536).astype(jnp.int32), bounds.astype(jnp.int32)


def add_tiles(table, first, last, adj, blocks, acc, masks):
    def step(s, carry):
        products = []
        for g in range(GROUPS):
            lhs, rhs = [], []
            for u in range(GROUP):
                e = table[(s * GROUPS + g) * GROUP + u]
                lhs.append(adj[e & 255])
                block = blocks[(e >> 8) & 255].reshape(8, 16, 128) * masks[(e >> 16) & 3][None]
                rhs.append(block.reshape(128, 128))
            products.append(
                jnp.dot(jnp.concatenate(lhs, axis=1), jnp.concatenate(rhs, axis=0), preferred_element_type=jnp.float32)
            )
        for g, product in enumerate(products):
            acc[table[(s * GROUPS + g) * GROUP] >> 18] += product
        return carry

    lax.fori_loop(first, last, step, 0)


def set_masks(masks):
    lane = lax.broadcasted_iota(jnp.int32, (16, 128), 1)
    masks[0] = jnp.where(lane < 64, 1.0, 0.0).astype(masks.dtype)
    masks[1] = jnp.where(lane < 64, 0.0, 1.0).astype(masks.dtype)
    masks[2] = jnp.zeros((16, 128), masks.dtype)
    return lax.broadcasted_iota(jnp.int32, (128, 128), 1)


def pre_kernel(grad_out, relu_mask, out):
    g = grad_out[...].astype(jnp.float32) * relu_mask[...].astype(jnp.float32)
    out[...] = jnp.concatenate([g[:, :256], g[:, 256:]], axis=0).T.astype(out.dtype)


def masked(grad_out, relu_mask):
    vmem = pl.BlockSpec(memory_space=pltpu.VMEM)
    return pl.pallas_call(
        pre_kernel,
        out_shape=jax.ShapeDtypeStruct((256, 128), jnp.bfloat16),
        in_specs=[vmem, vmem],
        out_specs=vmem,
        compiler_params=pltpu.CompilerParams(vmem_limit_bytes=4 * 1024 * 1024),
        name="masked",
    )(grad_out.T, relu_mask.T)


def add_sources(table, bounds, adj, sources, first, acc, masks):
    for k, source in enumerate(sources):
        add_tiles(table, bounds[first + k], bounds[first + k + 1], adj, source, acc, masks)


def first_kernel(table, bounds, adj, *refs):
    *sources, acc, masks = refs
    set_masks(masks)
    acc[...] = jnp.zeros_like(acc)
    add_sources(table, bounds, adj, sources, 0, acc, masks)


def middle_kernel(table, bounds, adj, *refs):
    *sources, before, acc, masks = refs
    set_masks(masks)
    acc[...] = before[...]
    add_sources(table, bounds, adj, sources, 2, acc, masks)


def last_kernel(table, bounds, adj, *refs):
    *sources, before, features, weights, out, out_a, out_b, out_c, partial, acc, masks = refs
    outs = (out, out_a, out_b, out_c)
    lane = set_masks(masks)
    acc[...] = before[...]
    add_sources(table, bounds, adj, sources, 6, acc, masks)
    agg = [acc[r] + pltpu.roll(acc[r], 64, 1) for r in range(4)]
    rounded = jnp.concatenate([v.astype(jnp.bfloat16) for v in agg], axis=0)
    product = jnp.dot(features[...], rounded, preferred_element_type=jnp.float32)
    low = lax.broadcasted_iota(jnp.int32, (64, 128), 1) < 64
    for p in range(2):
        partial[:, p, :] = jnp.where(low, product[p * 128 : p * 128 + 64], product[p * 128 + 64 : p * 128 + 128])
    for r in range(2):
        packed = jnp.where(lane < 64, agg[r], agg[r + 2]).astype(out.dtype)
        for ref in outs:
            ref[pl.ds(r * 128, 128), :] = packed
    for k, ref in enumerate(outs):
        lanes = pl.multiple_of((lax.axis_index("yl") ^ (k >> 1)) * 128, 128)
        of_chip = weights[:, pl.ds(lanes, 128)].astype(jnp.float32)
        first = (lax.axis_index("core") ^ (k & 1)) == 0
        of_core = jnp.where(low == first, of_chip, pltpu.roll(of_chip, 64, 1))
        ref[pl.ds(256, 64), :] = of_core.astype(ref.dtype)


def call(kernel, table, bounds, adj, sources, others, out_shape, keep_acc, name):
    smem = pl.BlockSpec(memory_space=pltpu.SMEM)
    vmem = pl.BlockSpec(memory_space=pltpu.VMEM)
    sources = [s.reshape(-1, 128, 128) for s in sources]
    return pl.pallas_call(
        kernel,
        out_shape=out_shape,
        in_specs=[smem, smem, vmem] + [vmem] * len(sources) + [vmem] * len(others),
        out_specs=jax.tree.map(lambda _: vmem, out_shape),
        scratch_shapes=([pltpu.VMEM((4, 128, 128), jnp.float32)] if keep_acc else []) + [
            pltpu.VMEM((3, 16, 128), jnp.bfloat16),
        ],
        compiler_params=pltpu.CompilerParams(vmem_limit_bytes=4 * 1024 * 1024),
        cost_estimate=pl.CostEstimate(flops=2 * 64 * 128 * 128 * 128, bytes_accessed=8 * 1024 * 1024, transcendentals=0),
        name=name,
    )(table, bounds, adj, *sources, *others)


def input_kernel(*refs):
    *messages, out = refs
    row = lax.broadcasted_iota(jnp.int32, (128, 128), 0)
    lane = lax.broadcasted_iota(jnp.int32, (128, 128), 1)
    factors = []
    for m in messages:
        block = m[pl.ds(256, 64), :].astype(jnp.float32)
        twice = jnp.concatenate([block, block], axis=0).T
        factors.append(jnp.where((row < 64) == (lane < 64), twice, 0.0).astype(jnp.bfloat16))
    sums = jnp.concatenate([m[pl.ds(0, 256), :] for m in messages], axis=1)
    result = lax.dot_general(
        jnp.concatenate(factors, axis=1), sums, (((1,), (1,)), ((), ())), preferred_element_type=jnp.float32
    )
    out[:, pl.ds(0, 256)] = result[:64].astype(out.dtype)
    out[:, pl.ds(256, 256)] = result[64:].astype(out.dtype)


def input_gradient(messages):
    vmem = pl.BlockSpec(memory_space=pltpu.VMEM)
    return pl.pallas_call(
        input_kernel,
        out_shape=jax.ShapeDtypeStruct((64, 512), jnp.bfloat16),
        in_specs=[vmem] * len(messages),
        out_specs=vmem,
        compiler_params=pltpu.CompilerParams(vmem_limit_bytes=4 * 1024 * 1024),
        cost_estimate=pl.CostEstimate(flops=2 * 128 * 512 * 256, bytes_accessed=400 * 1024, transcendentals=0),
        name="input_gradient",
    )(*messages)


def body(adj_tiles, tile_index, grad_out, relu_mask, features, weight):
    position = lax.axis_index(ROWS)
    source, place, half = where_held(tile_index[:, 1])
    low, high, position = gather_early(masked(grad_out, relu_mask), position)
    forwarded, others = gather_near(low, high)

    tables = tile_table(tile_index[:, 0] - position * 4, source, place, half, 8)
    f_rows = features.reshape(512, 64, 4).transpose(2, 1, 0).reshape(256, 512)
    low, high, tables, f_rows = lax.optimization_barrier((low, high, tables, f_rows))

    sums = jax.ShapeDtypeStruct((4, 128, 128), jnp.float32)
    acc = call(first_kernel, *tables, adj_tiles, [low, high], [], sums, False, "early_tiles")
    forwarded, acc = lax.optimization_barrier((forwarded, acc))
    far = gather_far(*forwarded)
    acc = call(middle_kernel, *tables, adj_tiles, forwarded + others, [acc], sums, False, "near_tiles")
    message = jax.ShapeDtypeStruct((320, 128), jnp.bfloat16)
    outs = (message, message, message, message, jax.ShapeDtypeStruct((64, 2, 128), jnp.float32))
    *messages, partial = call(last_kernel, *tables, adj_tiles, far, [acc, f_rows, weight.T], outs, True, "far_tiles")

    pieces = lax.all_to_all(partial, ROWS, 0, 0, tiled=True)
    arrived = messages[:1] + [lax.ppermute(m, SLAB, pairs) for m, pairs in zip(messages[1:], FLIPS)]
    grad_input = input_gradient(arrived).T
    total = jnp.sum(pieces, axis=0)
    grad_weight = jnp.concatenate([total[p : p + 1, k : k + 64] for p in range(2) for k in (0, 64)], axis=0)
    return grad_input, grad_weight


def solution(mesh):
    fine = Mesh(mesh.devices.reshape(NZ, NY, NX, NL, NC), ALL)
    return jax.shard_map(
        body,
        mesh=fine,
        in_specs=(P(ROWS, None, None), P(ROWS, None), P(ROWS, SLAB), P(ROWS, SLAB), P(ROWS, None), P(None, SLAB)),
        out_specs=(P(ROWS, SLAB), P(ROWS, SLAB)),
        check_vma=False,
    )
```

```python
import jax
import jax.numpy as jnp
from jax import lax
from jax.experimental import pallas as pl
from jax.experimental.pallas import tpu as pltpu
from jax.sharding import Mesh, PartitionSpec as P

NZ, NY, NX, NL, NC = 8, 2, 4, 2, 2
ROWS = ("z", "yh", "x")
SLAB = ("yl", "core")
ALL = ROWS + SLAB
GROUP = 4
GROUPS = 4
FLIPS = ([(0, 1), (1, 0), (2, 3), (3, 2)], [(0, 2), (2, 0), (1, 3), (3, 1)], [(0, 3), (3, 0), (1, 2), (2, 1)])


def device(z, y, x, l, c):
    return ((((z % NZ) * NY + y % NY) * NX + x % NX) * NL + l) * NC + c


def places():
    return [(z, y, x, l, c) for z in range(NZ) for y in range(NY) for x in range(NX) for l in range(NL) for c in range(NC)]


def from_rows(value, dz=0, dy=0):
    pairs = [(device(z + dz, y + dy, x, l, c), device(z, y, x, l, c)) for z, y, x, l, c in places()]
    return lax.ppermute(value, ALL, pairs)


def from_axis(value, second, step):
    pairs = []
    for z, y, x, l, c in places():
        along_x = (c == 0) != second
        z_step = -step if step == 2 and z % 2 else step
        source = device(z, y, x + step, l, c) if along_x else device(z + z_step, y, x, l, c)
        pairs.append((source, device(z, y, x, l, c)))
    return lax.ppermute(value, ALL, pairs)


def exchange(value, second_pairs):
    pairs = []
    for z, y, x, l, c in places():
        at = z if c == 0 else x
        step = 1 if (at % 2 == 0) != second_pairs else -1
        source = device(z + step, y, x, l, c) if c == 0 else device(z, y, x + step, l, c)
        pairs.append((source, device(z, y, x, l, c)))
    return lax.ppermute(value, ALL, pairs)


def odd_place():
    return jnp.where(lax.axis_index("core") == 0, lax.axis_index("z"), lax.axis_index("x")) % 2 == 1


def gather_early(packed, position):
    far_y, far = from_rows(packed, dz=4, dy=1), from_rows(packed, dz=4)
    again, position = lax.optimization_barrier((packed, position))
    four = jnp.stack([packed, from_rows(again, dy=1), far, far_y])
    high = jnp.stack([from_axis(four, False, -1), from_axis(four, False, 2)])
    low = jnp.stack([lax.optimization_barrier(four), from_axis(four, False, 1)])
    return low, high, position


def gather_near(low, high):
    odd = odd_place()
    forwarded = [from_axis(high, True, -1), from_axis(low, True, 1)]
    low, high = lax.optimization_barrier((low, high))
    others = [exchange(jnp.where(odd, high, low), False), exchange(jnp.where(odd, low, high), True)]
    return forwarded, others


def gather_far(minus, plus):
    return [from_axis(minus, True, -1), from_axis(plus, True, 1)]


def where_held(column):
    owner, block = column // 4, column % 4
    core = lax.axis_index("core")
    dz = (owner // (NY * NX) - lax.axis_index("z")) % NZ
    dy = (owner // NX - lax.axis_index("yh")) % NY
    dx = (owner - lax.axis_index("x")) % NX
    ring = jnp.where(core == 0, dx, dz % 4)
    late = jnp.where(core == 0, dz % 4, dx)
    a = jnp.where(ring == 2, 3, jnp.where(ring == 3, 2, ring))
    upper = (dz >= 3) & (dz <= 6)
    swapped = jnp.where(core == 0, (late == 2) & (a >= 2), (ring == 2) & (lax.axis_index("z") % 2 == 1))
    e = dy + 2 * (upper != swapped).astype(jnp.int32)
    high, odd = a // 2, odd_place().astype(jnp.int32)
    after = jnp.where(high == 0, 3, 4 + odd)
    before = jnp.where(high == 1, 2, 5 - odd)
    source = jnp.where(late == 0, 1 - high, jnp.where(late == 1, after, jnp.where(late == 3, before, 7 - high)))
    place = (a % 2 * 4 + e) * 2 + block % 2
    return source, place, block // 2


def tile_table(row, source, place, half, count):
    listed = row.shape[0]
    t = jnp.arange(listed)
    keys, sources = jnp.arange(count * 4), jnp.arange(count)
    key = source * 4 + row
    rank = jnp.sum(((key[None, :] == key[:, None]) & (t[None, :] < t[:, None])).astype(jnp.int32), axis=1)
    held = jnp.sum((key[:, None] == keys[None, :]).astype(jnp.int32), axis=0)
    need = (held + GROUP - 1) // GROUP
    total = jnp.sum(jnp.where(keys[None, :] // 4 == sources[:, None], need[None, :], 0), axis=1)
    turns = (total + GROUPS - 1) // GROUPS
    bounds = jnp.sum(jnp.where(sources[None, :] < jnp.arange(count + 1)[:, None], turns[None, :], 0), axis=1)
    ahead = (keys[None, :] // 4 == keys[:, None] // 4) & (keys[None, :] < keys[:, None])
    begin = jnp.sum(jnp.where(ahead, need[None, :], 0), axis=1)
    begin = begin + GROUPS * jnp.sum(jnp.where(keys[:, None] // 4 == sources[None, :], bounds[None, :count], 0), axis=1)
    group = jnp.sum(jnp.where(key[:, None] == keys[None, :], begin[None, :], 0), axis=1) + rank // GROUP
    slot = group * GROUP + rank % GROUP
    value = 1 + t + place * 256 + half * 65536 + row * 262144
    most = listed // (GROUP * GROUPS) + (3 * count + 1) // 2
    j = jnp.arange(most * GROUPS * GROUP)
    table = jnp.sum(jnp.where(slot[None, :] == j[:, None], value[None, :], 0), axis=1)
    return jnp.where(table > 0, table - 1, 2 * 65536).astype(jnp.int32), bounds.astype(jnp.int32)


def add_tiles(table, first, last, adj, blocks, acc, masks):
    def step(s, carry):
        products = []
        for g in range(GROUPS):
            lhs, rhs = [], []
            for u in range(GROUP):
                e = table[(s * GROUPS + g) * GROUP + u]
                lhs.append(adj[e & 255])
                block = blocks[(e >> 8) & 255].reshape(8, 16, 128) * masks[(e >> 16) & 3][None]
                rhs.append(block.reshape(128, 128))
            products.append(
                jnp.dot(jnp.concatenate(lhs, axis=1), jnp.concatenate(rhs, axis=0), preferred_element_type=jnp.float32)
            )
        for g, product in enumerate(products):
            acc[table[(s * GROUPS + g) * GROUP] >> 18] += product
        return carry

    lax.fori_loop(first, last, step, 0)


def set_masks(masks):
    lane = lax.broadcasted_iota(jnp.int32, (16, 128), 1)
    masks[0] = jnp.where(lane < 64, 1.0, 0.0).astype(masks.dtype)
    masks[1] = jnp.where(lane < 64, 0.0, 1.0).astype(masks.dtype)
    masks[2] = jnp.zeros((16, 128), masks.dtype)
    return lax.broadcasted_iota(jnp.int32, (128, 128), 1)


def pre_kernel(grad_out, relu_mask, out):
    g = grad_out[...].astype(jnp.float32) * relu_mask[...].astype(jnp.float32)
    out[...] = jnp.concatenate([g[:, :256], g[:, 256:]], axis=0).T.astype(out.dtype)


def masked(grad_out, relu_mask):
    vmem = pl.BlockSpec(memory_space=pltpu.VMEM)
    return pl.pallas_call(
        pre_kernel,
        out_shape=jax.ShapeDtypeStruct((256, 128), jnp.bfloat16),
        in_specs=[vmem, vmem],
        out_specs=vmem,
        compiler_params=pltpu.CompilerParams(vmem_limit_bytes=4 * 1024 * 1024),
        name="masked",
    )(grad_out.T, relu_mask.T)


def add_sources(table, bounds, adj, sources, first, acc, masks):
    for k, source in enumerate(sources):
        add_tiles(table, bounds[first + k], bounds[first + k + 1], adj, source, acc, masks)


def first_kernel(table, bounds, adj, *refs):
    *sources, acc, masks = refs
    set_masks(masks)
    acc[...] = jnp.zeros_like(acc)
    add_sources(table, bounds, adj, sources, 0, acc, masks)


def middle_kernel(table, bounds, adj, *refs):
    *sources, before, acc, masks = refs
    set_masks(masks)
    acc[...] = before[...]
    add_sources(table, bounds, adj, sources, 2, acc, masks)


def last_kernel(table, bounds, adj, *refs):
    *sources, before, features, weights, out, out_a, out_b, out_c, partial, acc, masks = refs
    outs = (out, out_a, out_b, out_c)
    lane = set_masks(masks)
    acc[...] = before[...]
    add_sources(table, bounds, adj, sources, 6, acc, masks)
    agg = [acc[r] + pltpu.roll(acc[r], 64, 1) for r in range(4)]
    rounded = jnp.concatenate([v.astype(jnp.bfloat16) for v in agg], axis=0)
    product = jnp.dot(features[...], rounded, preferred_element_type=jnp.float32)
    low = lax.broadcasted_iota(jnp.int32, (64, 128), 1) < 64
    for p in range(2):
        partial[:, p, :] = jnp.where(low, product[p * 128 : p * 128 + 64], product[p * 128 + 64 : p * 128 + 128])
    for r in range(2):
        packed = jnp.where(lane < 64, agg[r], agg[r + 2]).astype(out.dtype)
        for ref in outs:
            ref[pl.ds(r * 128, 128), :] = packed
    for k, ref in enumerate(outs):
        lanes = pl.multiple_of((lax.axis_index("yl") ^ (k >> 1)) * 128, 128)
        of_chip = weights[:, pl.ds(lanes, 128)].astype(jnp.float32)
        first = (lax.axis_index("core") ^ (k & 1)) == 0
        of_core = jnp.where(low == first, of_chip, pltpu.roll(of_chip, 64, 1))
        ref[pl.ds(256, 64), :] = of_core.astype(ref.dtype)


def call(kernel, table, bounds, adj, sources, others, out_shape, keep_acc, name):
    smem = pl.BlockSpec(memory_space=pltpu.SMEM)
    vmem = pl.BlockSpec(memory_space=pltpu.VMEM)
    sources = [s.reshape(-1, 128, 128) for s in sources]
    return pl.pallas_call(
        kernel,
        out_shape=out_shape,
        in_specs=[smem, smem, vmem] + [vmem] * len(sources) + [vmem] * len(others),
        out_specs=jax.tree.map(lambda _: vmem, out_shape),
        scratch_shapes=([pltpu.VMEM((4, 128, 128), jnp.float32)] if keep_acc else []) + [
            pltpu.VMEM((3, 16, 128), jnp.bfloat16),
        ],
        compiler_params=pltpu.CompilerParams(vmem_limit_bytes=4 * 1024 * 1024),
        cost_estimate=pl.CostEstimate(flops=2 * 64 * 128 * 128 * 128, bytes_accessed=8 * 1024 * 1024, transcendentals=0),
        name=name,
    )(table, bounds, adj, *sources, *others)


def input_kernel(*refs):
    *messages, out = refs
    row = lax.broadcasted_iota(jnp.int32, (128, 128), 0)
    lane = lax.broadcasted_iota(jnp.int32, (128, 128), 1)
    factors = []
    for m in messages:
        block = m[pl.ds(256, 64), :].astype(jnp.float32)
        twice = jnp.concatenate([block, block], axis=0).T
        factors.append(jnp.where((row < 64) == (lane < 64), twice, 0.0).astype(jnp.bfloat16))
    sums = jnp.concatenate([m[pl.ds(0, 256), :] for m in messages], axis=1)
    result = lax.dot_general(
        jnp.concatenate(factors, axis=1), sums, (((1,), (1,)), ((), ())), preferred_element_type=jnp.float32
    )
    out[:, pl.ds(0, 256)] = result[:64].astype(out.dtype)
    out[:, pl.ds(256, 256)] = result[64:].astype(out.dtype)


def input_gradient(messages):
    vmem = pl.BlockSpec(memory_space=pltpu.VMEM)
    return pl.pallas_call(
        input_kernel,
        out_shape=jax.ShapeDtypeStruct((64, 512), jnp.bfloat16),
        in_specs=[vmem] * len(messages),
        out_specs=vmem,
        compiler_params=pltpu.CompilerParams(vmem_limit_bytes=4 * 1024 * 1024),
        cost_estimate=pl.CostEstimate(flops=2 * 128 * 512 * 256, bytes_accessed=400 * 1024, transcendentals=0),
        name="input_gradient",
    )(*messages)


def body(adj_tiles, tile_index, grad_out, relu_mask, features, weight):
    position = lax.axis_index(ROWS)
    source, place, half = where_held(tile_index[:, 1])
    low, high, position = gather_early(masked(grad_out, relu_mask), position)
    forwarded, others = gather_near(low, high)

    tables = tile_table(tile_index[:, 0] - position * 4, source, place, half, 8)
    f_rows = features.reshape(512, 64, 4).transpose(2, 1, 0).reshape(256, 512)
    high, low, tables, f_rows = lax.optimization_barrier((high, low, tables, f_rows))

    sums = jax.ShapeDtypeStruct((4, 128, 128), jnp.float32)
    acc = call(first_kernel, *tables, adj_tiles, [high, low], [], sums, False, "early_tiles")
    forwarded, acc = lax.optimization_barrier((forwarded, acc))
    far = gather_far(*forwarded)
    acc = call(middle_kernel, *tables, adj_tiles, forwarded + others, [acc], sums, False, "near_tiles")
    message = jax.ShapeDtypeStruct((320, 128), jnp.bfloat16)
    outs = (message, message, message, message, jax.ShapeDtypeStruct((64, 2, 128), jnp.float32))
    *messages, partial = call(last_kernel, *tables, adj_tiles, far, [acc, f_rows, weight.T], outs, True, "far_tiles")

    pieces = lax.all_to_all(partial, ROWS, 0, 0, tiled=True)
    arrived = messages[:1] + [lax.ppermute(m, SLAB, pairs) for m, pairs in zip(messages[1:], FLIPS)]
    grad_input = input_gradient(arrived).T
    total = jnp.sum(pieces, axis=0)
    grad_weight = jnp.concatenate([total[p : p + 1, k : k + 64] for p in range(2) for k in (0, 64)], axis=0)
    return grad_input, grad_weight


def solution(mesh):
    fine = Mesh(mesh.devices.reshape(NZ, NY, NX, NL, NC), ALL)
    return jax.shard_map(
        body,
        mesh=fine,
        in_specs=(P(ROWS, None, None), P(ROWS, None), P(ROWS, SLAB), P(ROWS, SLAB), P(ROWS, None), P(None, SLAB)),
        out_specs=(P(ROWS, SLAB), P(ROWS, SLAB)),
        check_vma=False,
    )
```

```python
import jax
import jax.numpy as jnp
from jax import lax
from jax.experimental import pallas as pl
from jax.experimental.pallas import tpu as pltpu
from jax.experimental.layout import Layout, with_layout_constraint
from jax.sharding import Mesh, PartitionSpec as P

NZ, NY, NX, NL, NC = 8, 2, 4, 2, 2
ROWS = ("z", "yh", "x")
SLAB = ("yl", "core")
ALL = ROWS + SLAB
GROUP = 4
GROUPS = 4
FLIPS = ([(0, 1), (1, 0), (2, 3), (3, 2)], [(0, 2), (2, 0), (1, 3), (3, 1)], [(0, 3), (3, 0), (1, 2), (2, 1)])


def device(z, y, x, l, c):
    return ((((z % NZ) * NY + y % NY) * NX + x % NX) * NL + l) * NC + c


def places():
    return [(z, y, x, l, c) for z in range(NZ) for y in range(NY) for x in range(NX) for l in range(NL) for c in range(NC)]


def from_rows(value, dz=0, dy=0):
    pairs = [(device(z + dz, y + dy, x, l, c), device(z, y, x, l, c)) for z, y, x, l, c in places()]
    return lax.ppermute(value, ALL, pairs)


def from_axis(value, second, step):
    pairs = []
    for z, y, x, l, c in places():
        along_x = (c == 0) != second
        z_step = -step if step == 2 and z % 2 else step
        source = device(z, y, x + step, l, c) if along_x else device(z + z_step, y, x, l, c)
        pairs.append((source, device(z, y, x, l, c)))
    return lax.ppermute(value, ALL, pairs)


def exchange(value, second_pairs):
    pairs = []
    for z, y, x, l, c in places():
        at = z if c == 0 else x
        step = 1 if (at % 2 == 0) != second_pairs else -1
        source = device(z + step, y, x, l, c) if c == 0 else device(z, y, x + step, l, c)
        pairs.append((source, device(z, y, x, l, c)))
    return lax.ppermute(value, ALL, pairs)


def odd_place():
    return jnp.where(lax.axis_index("core") == 0, lax.axis_index("z"), lax.axis_index("x")) % 2 == 1


def gather_early(packed, position):
    far_y, far = from_rows(packed, dz=4, dy=1), from_rows(packed, dz=4)
    again, position = lax.optimization_barrier((packed, position))
    four = jnp.stack([packed, from_rows(again, dy=1), far, far_y])
    high = jnp.stack([from_axis(four, False, -1), from_axis(four, False, 2)])
    low = jnp.stack([lax.optimization_barrier(four), from_axis(four, False, 1)])
    return low, high, position


def gather_near(low, high):
    odd = odd_place()
    forwarded = [from_axis(high, True, -1), from_axis(low, True, 1)]
    low, high = lax.optimization_barrier((low, high))
    others = [exchange(jnp.where(odd, high, low), False), exchange(jnp.where(odd, low, high), True)]
    return forwarded, others


def gather_far(minus, plus):
    return [from_axis(minus, True, -1), from_axis(plus, True, 1)]


def where_held(column):
    owner, block = column // 4, column % 4
    core = lax.axis_index("core")
    dz = (owner // (NY * NX) - lax.axis_index("z")) % NZ
    dy = (owner // NX - lax.axis_index("yh")) % NY
    dx = (owner - lax.axis_index("x")) % NX
    ring = jnp.where(core == 0, dx, dz % 4)
    late = jnp.where(core == 0, dz % 4, dx)
    a = jnp.where(ring == 2, 3, jnp.where(ring == 3, 2, ring))
    upper = (dz >= 3) & (dz <= 6)
    swapped = jnp.where(core == 0, (late == 2) & (a >= 2), (ring == 2) & (lax.axis_index("z") % 2 == 1))
    e = dy + 2 * (upper != swapped).astype(jnp.int32)
    high, odd = a // 2, odd_place().astype(jnp.int32)
    after = jnp.where(high == 0, 3, 4 + odd)
    before = jnp.where(high == 1, 2, 5 - odd)
    source = jnp.where(late == 0, 1 - high, jnp.where(late == 1, after, jnp.where(late == 3, before, 7 - high)))
    place = (a % 2 * 4 + e) * 2 + block % 2
    return source, place, block // 2


def tile_table(row, source, place, half, count):
    listed = row.shape[0]
    t = jnp.arange(listed)
    keys, sources = jnp.arange(count * 4), jnp.arange(count)
    key = source * 4 + row
    rank = jnp.sum(((key[None, :] == key[:, None]) & (t[None, :] < t[:, None])).astype(jnp.int32), axis=1)
    held = jnp.sum((key[:, None] == keys[None, :]).astype(jnp.int32), axis=0)
    need = (held + GROUP - 1) // GROUP
    total = jnp.sum(jnp.where(keys[None, :] // 4 == sources[:, None], need[None, :], 0), axis=1)
    turns = (total + GROUPS - 1) // GROUPS
    bounds = jnp.sum(jnp.where(sources[None, :] < jnp.arange(count + 1)[:, None], turns[None, :], 0), axis=1)
    ahead = (keys[None, :] // 4 == keys[:, None] // 4) & (keys[None, :] < keys[:, None])
    begin = jnp.sum(jnp.where(ahead, need[None, :], 0), axis=1)
    begin = begin + GROUPS * jnp.sum(jnp.where(keys[:, None] // 4 == sources[None, :], bounds[None, :count], 0), axis=1)
    group = jnp.sum(jnp.where(key[:, None] == keys[None, :], begin[None, :], 0), axis=1) + rank // GROUP
    slot = group * GROUP + rank % GROUP
    value = 1 + t + place * 256 + half * 65536 + row * 262144
    most = listed // (GROUP * GROUPS) + (3 * count + 1) // 2
    j = jnp.arange(most * GROUPS * GROUP)
    table = jnp.sum(jnp.where(slot[None, :] == j[:, None], value[None, :], 0), axis=1)
    return jnp.where(table > 0, table - 1, 2 * 65536).astype(jnp.int32), bounds.astype(jnp.int32)


def add_tiles(table, first, last, adj, blocks, acc, masks):
    def step(s, carry):
        products = []
        for g in range(GROUPS):
            lhs, rhs = [], []
            for u in range(GROUP):
                e = table[(s * GROUPS + g) * GROUP + u]
                lhs.append(adj[e & 255])
                block = blocks[(e >> 8) & 255].reshape(8, 16, 128) * masks[(e >> 16) & 3][None]
                rhs.append(block.reshape(128, 128))
            products.append(
                jnp.dot(jnp.concatenate(lhs, axis=1), jnp.concatenate(rhs, axis=0), preferred_element_type=jnp.float32)
            )
        for g, product in enumerate(products):
            acc[table[(s * GROUPS + g) * GROUP] >> 18] += product
        return carry

    lax.fori_loop(first, last, step, 0)


def set_masks(masks):
    lane = lax.broadcasted_iota(jnp.int32, (16, 128), 1)
    masks[0] = jnp.where(lane < 64, 1.0, 0.0).astype(masks.dtype)
    masks[1] = jnp.where(lane < 64, 0.0, 1.0).astype(masks.dtype)
    masks[2] = jnp.zeros((16, 128), masks.dtype)
    return lax.broadcasted_iota(jnp.int32, (128, 128), 1)


def masked(grad_out, relu_mask):
    g_pre = (grad_out.T.astype(jnp.float32) * relu_mask.T.astype(jnp.float32)).astype(jnp.bfloat16)
    turned = with_layout_constraint(jnp.concatenate([g_pre[:, :256], g_pre[:, 256:]], axis=0), Layout((0, 1)))
    return with_layout_constraint(turned.T, Layout((0, 1)))


def add_sources(table, bounds, adj, sources, first, acc, masks):
    for k, source in enumerate(sources):
        add_tiles(table, bounds[first + k], bounds[first + k + 1], adj, source, acc, masks)


def first_kernel(table, bounds, adj, *refs):
    *sources, acc, masks = refs
    set_masks(masks)
    acc[...] = jnp.zeros_like(acc)
    add_sources(table, bounds, adj, sources, 0, acc, masks)


def middle_kernel(table, bounds, adj, *refs):
    *sources, before, acc, masks = refs
    set_masks(masks)
    acc[...] = before[...]
    add_sources(table, bounds, adj, sources, 2, acc, masks)


def last_kernel(table, bounds, adj, *refs):
    *sources, before, features, weights, out, out_a, out_b, out_c, partial, acc, masks = refs
    outs = (out, out_a, out_b, out_c)
    lane = set_masks(masks)
    acc[...] = before[...]
    add_sources(table, bounds, adj, sources, 6, acc, masks)
    agg = [acc[r] + pltpu.roll(acc[r], 64, 1) for r in range(4)]
    rounded = jnp.concatenate([v.astype(jnp.bfloat16) for v in agg], axis=0)
    product = jnp.dot(features[...], rounded, preferred_element_type=jnp.float32)
    low = lax.broadcasted_iota(jnp.int32, (64, 128), 1) < 64
    for p in range(2):
        partial[:, p, :] = jnp.where(low, product[p * 128 : p * 128 + 64], product[p * 128 + 64 : p * 128 + 128])
    for r in range(2):
        packed = jnp.where(lane < 64, agg[r], agg[r + 2]).astype(out.dtype)
        for ref in outs:
            ref[pl.ds(r * 128, 128), :] = packed
    for k, ref in enumerate(outs):
        lanes = pl.multiple_of((lax.axis_index("yl") ^ (k >> 1)) * 128, 128)
        of_chip = weights[:, pl.ds(lanes, 128)].astype(jnp.float32)
        first = (lax.axis_index("core") ^ (k & 1)) == 0
        of_core = jnp.where(low == first, of_chip, pltpu.roll(of_chip, 64, 1))
        ref[pl.ds(256, 64), :] = of_core.astype(ref.dtype)


def call(kernel, table, bounds, adj, sources, others, out_shape, keep_acc, name):
    smem = pl.BlockSpec(memory_space=pltpu.SMEM)
    vmem = pl.BlockSpec(memory_space=pltpu.VMEM)
    sources = [s.reshape(-1, 128, 128) for s in sources]
    return pl.pallas_call(
        kernel,
        out_shape=out_shape,
        in_specs=[smem, smem, vmem] + [vmem] * len(sources) + [vmem] * len(others),
        out_specs=jax.tree.map(lambda _: vmem, out_shape),
        scratch_shapes=([pltpu.VMEM((4, 128, 128), jnp.float32)] if keep_acc else []) + [
            pltpu.VMEM((3, 16, 128), jnp.bfloat16),
        ],
        compiler_params=pltpu.CompilerParams(vmem_limit_bytes=4 * 1024 * 1024),
        cost_estimate=pl.CostEstimate(flops=2 * 64 * 128 * 128 * 128, bytes_accessed=8 * 1024 * 1024, transcendentals=0),
        name=name,
    )(table, bounds, adj, *sources, *others)


def input_kernel(*refs):
    *messages, out = refs
    row = lax.broadcasted_iota(jnp.int32, (128, 128), 0)
    lane = lax.broadcasted_iota(jnp.int32, (128, 128), 1)
    factors = []
    for m in messages:
        block = m[pl.ds(256, 64), :].astype(jnp.float32)
        twice = jnp.concatenate([block, block], axis=0).T
        factors.append(jnp.where((row < 64) == (lane < 64), twice, 0.0).astype(jnp.bfloat16))
    sums = jnp.concatenate([m[pl.ds(0, 256), :] for m in messages], axis=1)
    result = lax.dot_general(
        jnp.concatenate(factors, axis=1), sums, (((1,), (1,)), ((), ())), preferred_element_type=jnp.float32
    )
    out[:, pl.ds(0, 256)] = result[:64].astype(out.dtype)
    out[:, pl.ds(256, 256)] = result[64:].astype(out.dtype)


def input_gradient(messages):
    vmem = pl.BlockSpec(memory_space=pltpu.VMEM)
    return pl.pallas_call(
        input_kernel,
        out_shape=jax.ShapeDtypeStruct((64, 512), jnp.bfloat16),
        in_specs=[vmem] * len(messages),
        out_specs=vmem,
        compiler_params=pltpu.CompilerParams(vmem_limit_bytes=4 * 1024 * 1024),
        cost_estimate=pl.CostEstimate(flops=2 * 128 * 512 * 256, bytes_accessed=400 * 1024, transcendentals=0),
        name="input_gradient",
    )(*messages)


def body(adj_tiles, tile_index, grad_out, relu_mask, features, weight):
    position = lax.axis_index(ROWS)
    source, place, half = where_held(tile_index[:, 1])
    low, high, position = gather_early(masked(grad_out, relu_mask), position)
    forwarded, others = gather_near(low, high)

    tables = tile_table(tile_index[:, 0] - position * 4, source, place, half, 8)
    f_rows = features.reshape(512, 64, 4).transpose(2, 1, 0).reshape(256, 512)
    high, low, tables, f_rows = lax.optimization_barrier((high, low, tables, f_rows))

    sums = jax.ShapeDtypeStruct((4, 128, 128), jnp.float32)
    acc = call(first_kernel, *tables, adj_tiles, [high, low], [], sums, False, "early_tiles")
    forwarded, acc = lax.optimization_barrier((forwarded, acc))
    far = gather_far(*forwarded)
    acc = call(middle_kernel, *tables, adj_tiles, forwarded + others, [acc], sums, False, "near_tiles")
    message = jax.ShapeDtypeStruct((320, 128), jnp.bfloat16)
    outs = (message, message, message, message, jax.ShapeDtypeStruct((64, 2, 128), jnp.float32))
    *messages, partial = call(last_kernel, *tables, adj_tiles, far, [acc, f_rows, weight.T], outs, True, "far_tiles")

    pieces = lax.all_to_all(partial, ROWS, 0, 0, tiled=True)
    arrived = messages[:1] + [lax.ppermute(m, SLAB, pairs) for m, pairs in zip(messages[1:], FLIPS)]
    grad_input = input_gradient(arrived).T
    total = jnp.sum(pieces, axis=0)
    grad_weight = jnp.concatenate([total[p : p + 1, k : k + 64] for p in range(2) for k in (0, 64)], axis=0)
    return grad_input, grad_weight


def solution(mesh):
    fine = Mesh(mesh.devices.reshape(NZ, NY, NX, NL, NC), ALL)
    return jax.shard_map(
        body,
        mesh=fine,
        in_specs=(P(ROWS, None, None), P(ROWS, None), P(ROWS, SLAB), P(ROWS, SLAB), P(ROWS, None), P(None, SLAB)),
        out_specs=(P(ROWS, SLAB), P(ROWS, SLAB)),
        check_vma=False,
    )
```

```python
import jax
import jax.numpy as jnp
from jax import lax
from jax.experimental import pallas as pl
from jax.experimental.pallas import tpu as pltpu
from jax.experimental.layout import Layout, with_layout_constraint
from jax.sharding import Mesh, PartitionSpec as P

NZ, NY, NX, NL, NC = 8, 2, 4, 2, 2
ROWS = ("z", "yh", "x")
SLAB = ("yl", "core")
ALL = ROWS + SLAB
GROUP = 4
GROUPS = 4
FLIPS = ([(0, 1), (1, 0), (2, 3), (3, 2)], [(0, 2), (2, 0), (1, 3), (3, 1)], [(0, 3), (3, 0), (1, 2), (2, 1)])


def device(z, y, x, l, c):
    return ((((z % NZ) * NY + y % NY) * NX + x % NX) * NL + l) * NC + c


def places():
    return [(z, y, x, l, c) for z in range(NZ) for y in range(NY) for x in range(NX) for l in range(NL) for c in range(NC)]


def from_rows(value, dz=0, dy=0):
    pairs = [(device(z + dz, y + dy, x, l, c), device(z, y, x, l, c)) for z, y, x, l, c in places()]
    return lax.ppermute(value, ALL, pairs)


def from_axis(value, second, step):
    pairs = []
    for z, y, x, l, c in places():
        along_x = (c == 0) != second
        z_step = -step if step == 2 and z % 2 else step
        source = device(z, y, x + step, l, c) if along_x else device(z + z_step, y, x, l, c)
        pairs.append((source, device(z, y, x, l, c)))
    return lax.ppermute(value, ALL, pairs)


def exchange(value, second_pairs):
    pairs = []
    for z, y, x, l, c in places():
        at = z if c == 0 else x
        step = 1 if (at % 2 == 0) != second_pairs else -1
        source = device(z + step, y, x, l, c) if c == 0 else device(z, y, x + step, l, c)
        pairs.append((source, device(z, y, x, l, c)))
    return lax.ppermute(value, ALL, pairs)


def odd_place():
    return jnp.where(lax.axis_index("core") == 0, lax.axis_index("z"), lax.axis_index("x")) % 2 == 1


def gather_early(packed, position):
    far_y, far = from_rows(packed, dz=4, dy=1), from_rows(packed, dz=4)
    again, position = lax.optimization_barrier((packed, position))
    four = jnp.stack([packed, from_rows(again, dy=1), far, far_y])
    high = jnp.stack([from_axis(four, False, -1), from_axis(four, False, 2)])
    low = jnp.stack([lax.optimization_barrier(four), from_axis(four, False, 1)])
    return low, high, position


def gather_near(low, high):
    odd = odd_place()
    minus = from_axis(high, True, -1)
    forwarded = [from_axis(low, True, 1), minus]
    low, high = lax.optimization_barrier((low, high))
    others = [exchange(jnp.where(odd, high, low), False), exchange(jnp.where(odd, low, high), True)]
    return forwarded, others


def gather_far(plus, minus):
    return [from_axis(plus, True, 1), from_axis(minus, True, -1)]


def where_held(column):
    owner, block = column // 4, column % 4
    core = lax.axis_index("core")
    dz = (owner // (NY * NX) - lax.axis_index("z")) % NZ
    dy = (owner // NX - lax.axis_index("yh")) % NY
    dx = (owner - lax.axis_index("x")) % NX
    ring = jnp.where(core == 0, dx, dz % 4)
    late = jnp.where(core == 0, dz % 4, dx)
    a = jnp.where(ring == 2, 3, jnp.where(ring == 3, 2, ring))
    upper = (dz >= 3) & (dz <= 6)
    swapped = jnp.where(core == 0, (late == 2) & (a >= 2), (ring == 2) & (lax.axis_index("z") % 2 == 1))
    e = dy + 2 * (upper != swapped).astype(jnp.int32)
    high, odd = a // 2, odd_place().astype(jnp.int32)
    after = jnp.where(high == 0, 2, 4 + odd)
    before = jnp.where(high == 1, 3, 5 - odd)
    source = jnp.where(late == 0, high, jnp.where(late == 1, after, jnp.where(late == 3, before, 6 + high)))
    place = (a % 2 * 4 + e) * 2 + block % 2
    return source, place, block // 2


def tile_table(row, source, place, half, count):
    listed = row.shape[0]
    t = jnp.arange(listed)
    keys, sources = jnp.arange(count * 4), jnp.arange(count)
    key = source * 4 + row
    rank = jnp.sum(((key[None, :] == key[:, None]) & (t[None, :] < t[:, None])).astype(jnp.int32), axis=1)
    held = jnp.sum((key[:, None] == keys[None, :]).astype(jnp.int32), axis=0)
    need = (held + GROUP - 1) // GROUP
    total = jnp.sum(jnp.where(keys[None, :] // 4 == sources[:, None], need[None, :], 0), axis=1)
    turns = (total + GROUPS - 1) // GROUPS
    bounds = jnp.sum(jnp.where(sources[None, :] < jnp.arange(count + 1)[:, None], turns[None, :], 0), axis=1)
    ahead = (keys[None, :] // 4 == keys[:, None] // 4) & (keys[None, :] < keys[:, None])
    begin = jnp.sum(jnp.where(ahead, need[None, :], 0), axis=1)
    begin = begin + GROUPS * jnp.sum(jnp.where(keys[:, None] // 4 == sources[None, :], bounds[None, :count], 0), axis=1)
    group = jnp.sum(jnp.where(key[:, None] == keys[None, :], begin[None, :], 0), axis=1) + rank // GROUP
    slot = group * GROUP + rank % GROUP
    value = 1 + t + place * 256 + half * 65536 + row * 262144
    most = listed // (GROUP * GROUPS) + (3 * count + 1) // 2
    j = jnp.arange(most * GROUPS * GROUP)
    table = jnp.sum(jnp.where(slot[None, :] == j[:, None], value[None, :], 0), axis=1)
    return jnp.where(table > 0, table - 1, 2 * 65536).astype(jnp.int32), bounds.astype(jnp.int32)


def add_tiles(table, first, last, adj, blocks, acc, masks):
    def step(s, carry):
        products = []
        for g in range(GROUPS):
            lhs, rhs = [], []
            for u in range(GROUP):
                e = table[(s * GROUPS + g) * GROUP + u]
                lhs.append(adj[e & 255])
                block = blocks[(e >> 8) & 255].reshape(8, 16, 128) * masks[(e >> 16) & 3][None]
                rhs.append(block.reshape(128, 128))
            products.append(
                jnp.dot(jnp.concatenate(lhs, axis=1), jnp.concatenate(rhs, axis=0), preferred_element_type=jnp.float32)
            )
        for g, product in enumerate(products):
            acc[table[(s * GROUPS + g) * GROUP] >> 18] += product
        return carry

    lax.fori_loop(first, last, step, 0)


def set_masks(masks):
    lane = lax.broadcasted_iota(jnp.int32, (16, 128), 1)
    masks[0] = jnp.where(lane < 64, 1.0, 0.0).astype(masks.dtype)
    masks[1] = jnp.where(lane < 64, 0.0, 1.0).astype(masks.dtype)
    masks[2] = jnp.zeros((16, 128), masks.dtype)
    return lax.broadcasted_iota(jnp.int32, (128, 128), 1)


def masked(grad_out, relu_mask):
    g_pre = (grad_out.T.astype(jnp.float32) * relu_mask.T.astype(jnp.float32)).astype(jnp.bfloat16)
    turned = with_layout_constraint(jnp.concatenate([g_pre[:, :256], g_pre[:, 256:]], axis=0), Layout((0, 1)))
    return with_layout_constraint(turned.T, Layout((0, 1)))


def add_sources(table, bounds, adj, sources, first, acc, masks):
    for k, source in enumerate(sources):
        add_tiles(table, bounds[first + k], bounds[first + k + 1], adj, source, acc, masks)


def first_kernel(table, bounds, adj, *refs):
    *sources, acc, masks = refs
    set_masks(masks)
    acc[...] = jnp.zeros_like(acc)
    add_sources(table, bounds, adj, sources, 0, acc, masks)


def middle_kernel(table, bounds, adj, *refs):
    *sources, before, acc, masks = refs
    set_masks(masks)
    acc[...] = before[...]
    add_sources(table, bounds, adj, sources, 2, acc, masks)


def last_kernel(table, bounds, adj, *refs):
    *sources, before, features, weights, out, out_a, out_b, out_c, partial, acc, masks = refs
    outs = (out, out_a, out_b, out_c)
    lane = set_masks(masks)
    acc[...] = before[...]
    add_sources(table, bounds, adj, sources, 6, acc, masks)
    agg = [acc[r] + pltpu.roll(acc[r], 64, 1) for r in range(4)]
    rounded = jnp.concatenate([v.astype(jnp.bfloat16) for v in agg], axis=0)
    product = jnp.dot(features[...], rounded, preferred_element_type=jnp.float32)
    low = lax.broadcasted_iota(jnp.int32, (64, 128), 1) < 64
    for p in range(2):
        partial[:, p, :] = jnp.where(low, product[p * 128 : p * 128 + 64], product[p * 128 + 64 : p * 128 + 128])
    for r in range(2):
        packed = jnp.where(lane < 64, agg[r], agg[r + 2]).astype(out.dtype)
        for ref in outs:
            ref[pl.ds(r * 128, 128), :] = packed
    for k, ref in enumerate(outs):
        lanes = pl.multiple_of((lax.axis_index("yl") ^ (k >> 1)) * 128, 128)
        of_chip = weights[:, pl.ds(lanes, 128)].astype(jnp.float32)
        first = (lax.axis_index("core") ^ (k & 1)) == 0
        of_core = jnp.where(low == first, of_chip, pltpu.roll(of_chip, 64, 1))
        ref[pl.ds(256, 64), :] = of_core.astype(ref.dtype)


def call(kernel, table, bounds, adj, sources, others, out_shape, keep_acc, name):
    smem = pl.BlockSpec(memory_space=pltpu.SMEM)
    vmem = pl.BlockSpec(memory_space=pltpu.VMEM)
    sources = [s.reshape(-1, 128, 128) for s in sources]
    return pl.pallas_call(
        kernel,
        out_shape=out_shape,
        in_specs=[smem, smem, vmem] + [vmem] * len(sources) + [vmem] * len(others),
        out_specs=jax.tree.map(lambda _: vmem, out_shape),
        scratch_shapes=([pltpu.VMEM((4, 128, 128), jnp.float32)] if keep_acc else []) + [
            pltpu.VMEM((3, 16, 128), jnp.bfloat16),
        ],
        compiler_params=pltpu.CompilerParams(vmem_limit_bytes=4 * 1024 * 1024),
        cost_estimate=pl.CostEstimate(flops=2 * 64 * 128 * 128 * 128, bytes_accessed=8 * 1024 * 1024, transcendentals=0),
        name=name,
    )(table, bounds, adj, *sources, *others)


def input_kernel(*refs):
    *messages, out = refs
    row = lax.broadcasted_iota(jnp.int32, (128, 128), 0)
    lane = lax.broadcasted_iota(jnp.int32, (128, 128), 1)
    factors = []
    for m in messages:
        block = m[pl.ds(256, 64), :].astype(jnp.float32)
        twice = jnp.concatenate([block, block], axis=0).T
        factors.append(jnp.where((row < 64) == (lane < 64), twice, 0.0).astype(jnp.bfloat16))
    sums = jnp.concatenate([m[pl.ds(0, 256), :] for m in messages], axis=1)
    result = lax.dot_general(
        jnp.concatenate(factors, axis=1), sums, (((1,), (1,)), ((), ())), preferred_element_type=jnp.float32
    )
    out[:, pl.ds(0, 256)] = result[:64].astype(out.dtype)
    out[:, pl.ds(256, 256)] = result[64:].astype(out.dtype)


def input_gradient(messages):
    vmem = pl.BlockSpec(memory_space=pltpu.VMEM)
    return pl.pallas_call(
        input_kernel,
        out_shape=jax.ShapeDtypeStruct((64, 512), jnp.bfloat16),
        in_specs=[vmem] * len(messages),
        out_specs=vmem,
        compiler_params=pltpu.CompilerParams(vmem_limit_bytes=4 * 1024 * 1024),
        cost_estimate=pl.CostEstimate(flops=2 * 128 * 512 * 256, bytes_accessed=400 * 1024, transcendentals=0),
        name="input_gradient",
    )(*messages)


def body(adj_tiles, tile_index, grad_out, relu_mask, features, weight):
    position = lax.axis_index(ROWS)
    source, place, half = where_held(tile_index[:, 1])
    low, high, position = gather_early(masked(grad_out, relu_mask), position)
    forwarded, others = gather_near(low, high)

    tables = tile_table(tile_index[:, 0] - position * 4, source, place, half, 8)
    f_rows = features.reshape(512, 64, 4).transpose(2, 1, 0).reshape(256, 512)
    low, high, tables, f_rows = lax.optimization_barrier((low, high, tables, f_rows))

    sums = jax.ShapeDtypeStruct((4, 128, 128), jnp.float32)
    acc = call(first_kernel, *tables, adj_tiles, [low, high], [], sums, False, "early_tiles")
    forwarded, acc = lax.optimization_barrier((forwarded, acc))
    far = gather_far(*forwarded)
    acc = call(middle_kernel, *tables, adj_tiles, forwarded + others, [acc], sums, False, "near_tiles")
    message = jax.ShapeDtypeStruct((320, 128), jnp.bfloat16)
    outs = (message, message, message, message, jax.ShapeDtypeStruct((64, 2, 128), jnp.float32))
    *messages, partial = call(last_kernel, *tables, adj_tiles, far, [acc, f_rows, weight.T], outs, True, "far_tiles")

    pieces = lax.all_to_all(partial, ROWS, 0, 0, tiled=True)
    arrived = messages[:1] + [lax.ppermute(m, SLAB, pairs) for m, pairs in zip(messages[1:], FLIPS)]
    grad_input = input_gradient(arrived).T
    total = jnp.sum(pieces, axis=0)
    grad_weight = jnp.concatenate([total[p : p + 1, k : k + 64] for p in range(2) for k in (0, 64)], axis=0)
    return grad_input, grad_weight


def solution(mesh):
    fine = Mesh(mesh.devices.reshape(NZ, NY, NX, NL, NC), ALL)
    return jax.shard_map(
        body,
        mesh=fine,
        in_specs=(P(ROWS, None, None), P(ROWS, None), P(ROWS, SLAB), P(ROWS, SLAB), P(ROWS, None), P(None, SLAB)),
        out_specs=(P(ROWS, SLAB), P(ROWS, SLAB)),
        check_vma=False,
    )
```

```python
import jax
import jax.numpy as jnp
from jax import lax
from jax.experimental import pallas as pl
from jax.experimental.pallas import tpu as pltpu
from jax.experimental.layout import Layout, with_layout_constraint
from jax.sharding import Mesh, PartitionSpec as P

NZ, NY, NX, NL, NC = 8, 2, 4, 2, 2
ROWS = ("z", "yh", "x")
SLAB = ("yl", "core")
ALL = ROWS + SLAB
GROUP = 4
GROUPS = 4
FLIPS = ([(0, 1), (1, 0), (2, 3), (3, 2)], [(0, 2), (2, 0), (1, 3), (3, 1)], [(0, 3), (3, 0), (1, 2), (2, 1)])


def device(z, y, x, l, c):
    return ((((z % NZ) * NY + y % NY) * NX + x % NX) * NL + l) * NC + c


def places():
    return [(z, y, x, l, c) for z in range(NZ) for y in range(NY) for x in range(NX) for l in range(NL) for c in range(NC)]


def from_rows(value, dz=0, dy=0):
    pairs = [(device(z + dz, y + dy, x, l, c), device(z, y, x, l, c)) for z, y, x, l, c in places()]
    return lax.ppermute(value, ALL, pairs)


def from_axis(value, second, step):
    pairs = []
    for z, y, x, l, c in places():
        along_x = (c == 0) != second
        z_step = -step if step == 2 and z % 2 else step
        source = device(z, y, x + step, l, c) if along_x else device(z + z_step, y, x, l, c)
        pairs.append((source, device(z, y, x, l, c)))
    return lax.ppermute(value, ALL, pairs)


def exchange(value, second_pairs):
    pairs = []
    for z, y, x, l, c in places():
        at = z if c == 0 else x
        step = 1 if (at % 2 == 0) != second_pairs else -1
        source = device(z + step, y, x, l, c) if c == 0 else device(z, y, x + step, l, c)
        pairs.append((source, device(z, y, x, l, c)))
    return lax.ppermute(value, ALL, pairs)


def odd_place():
    return jnp.where(lax.axis_index("core") == 0, lax.axis_index("z"), lax.axis_index("x")) % 2 == 1


def gather_early(packed, position):
    far_y, far = from_rows(packed, dz=4, dy=1), from_rows(packed, dz=4)
    again, position = lax.optimization_barrier((packed, position))
    four = jnp.stack([packed, from_rows(again, dy=1), far, far_y])
    high = jnp.stack([from_axis(four, False, -1), from_axis(four, False, 2)])
    low = jnp.stack([lax.optimization_barrier(four), from_axis(four, False, 1)])
    return low, high, position


def gather_near(low, high):
    odd = odd_place()
    minus = from_axis(high, True, -1)
    forwarded = [from_axis(low, True, 1), minus]
    low, high = lax.optimization_barrier((low, high))
    others = [exchange(jnp.where(odd, high, low), False), exchange(jnp.where(odd, low, high), True)]
    return forwarded, others


def gather_far(plus, minus):
    return [from_axis(plus, True, 1), from_axis(minus, True, -1)]


def where_held(column):
    owner, block = column // 4, column % 4
    core = lax.axis_index("core")
    dz = (owner // (NY * NX) - lax.axis_index("z")) % NZ
    dy = (owner // NX - lax.axis_index("yh")) % NY
    dx = (owner - lax.axis_index("x")) % NX
    ring = jnp.where(core == 0, dx, dz % 4)
    late = jnp.where(core == 0, dz % 4, dx)
    a = jnp.where(ring == 2, 3, jnp.where(ring == 3, 2, ring))
    upper = (dz >= 3) & (dz <= 6)
    swapped = jnp.where(core == 0, (late == 2) & (a >= 2), (ring == 2) & (lax.axis_index("z") % 2 == 1))
    e = dy + 2 * (upper != swapped).astype(jnp.int32)
    high, odd = a // 2, odd_place().astype(jnp.int32)
    after = jnp.where(high == 0, 2, 4 + odd)
    before = jnp.where(high == 1, 3, 5 - odd)
    source = jnp.where(late == 0, high, jnp.where(late == 1, after, jnp.where(late == 3, before, 6 + high)))
    place = (a % 2 * 4 + e) * 2 + block % 2
    return source, place, block // 2


def tile_table(row, source, place, half, count):
    listed = row.shape[0]
    t = jnp.arange(listed)
    keys, sources = jnp.arange(count * 4), jnp.arange(count)
    key = source * 4 + row
    rank = jnp.sum(((key[None, :] == key[:, None]) & (t[None, :] < t[:, None])).astype(jnp.int32), axis=1)
    held = jnp.sum((key[:, None] == keys[None, :]).astype(jnp.int32), axis=0)
    need = (held + GROUP - 1) // GROUP
    total = jnp.sum(jnp.where(keys[None, :] // 4 == sources[:, None], need[None, :], 0), axis=1)
    turns = (total + GROUPS - 1) // GROUPS
    bounds = jnp.sum(jnp.where(sources[None, :] < jnp.arange(count + 1)[:, None], turns[None, :], 0), axis=1)
    ahead = (keys[None, :] // 4 == keys[:, None] // 4) & (keys[None, :] < keys[:, None])
    begin = jnp.sum(jnp.where(ahead, need[None, :], 0), axis=1)
    begin = begin + GROUPS * jnp.sum(jnp.where(keys[:, None] // 4 == sources[None, :], bounds[None, :count], 0), axis=1)
    group = jnp.sum(jnp.where(key[:, None] == keys[None, :], begin[None, :], 0), axis=1) + rank // GROUP
    slot = group * GROUP + rank % GROUP
    value = 1 + t + place * 256 + half * 65536 + row * 262144
    most = listed // (GROUP * GROUPS) + (3 * count + 1) // 2
    j = jnp.arange(most * GROUPS * GROUP)
    table = jnp.sum(jnp.where(slot[None, :] == j[:, None], value[None, :], 0), axis=1)
    return jnp.where(table > 0, table - 1, 2 * 65536).astype(jnp.int32), bounds.astype(jnp.int32)


def add_tiles(table, first, last, adj, blocks, acc, masks):
    def step(s, carry):
        products = []
        for g in range(GROUPS):
            lhs, rhs = [], []
            for u in range(GROUP):
                e = table[(s * GROUPS + g) * GROUP + u]
                lhs.append(adj[e & 255])
                block = blocks[(e >> 8) & 255].reshape(8, 16, 128) * masks[(e >> 16) & 3][None]
                rhs.append(block.reshape(128, 128))
            products.append(
                jnp.dot(jnp.concatenate(lhs, axis=1), jnp.concatenate(rhs, axis=0), preferred_element_type=jnp.float32)
            )
        for g, product in enumerate(products):
            acc[table[(s * GROUPS + g) * GROUP] >> 18] += product
        return carry

    lax.fori_loop(first, last, step, 0)


def set_masks(masks):
    lane = lax.broadcasted_iota(jnp.int32, (16, 128), 1)
    masks[0] = jnp.where(lane < 64, 1.0, 0.0).astype(masks.dtype)
    masks[1] = jnp.where(lane < 64, 0.0, 1.0).astype(masks.dtype)
    masks[2] = jnp.zeros((16, 128), masks.dtype)
    return lax.broadcasted_iota(jnp.int32, (128, 128), 1)


def masked(grad_out, relu_mask):
    g_pre = (grad_out.T.astype(jnp.float32) * relu_mask.T.astype(jnp.float32)).astype(jnp.bfloat16)
    turned = with_layout_constraint(jnp.concatenate([g_pre[:, :256], g_pre[:, 256:]], axis=0), Layout((0, 1)))
    return with_layout_constraint(turned.T, Layout((0, 1)))


def add_sources(table, bounds, adj, sources, first, acc, masks):
    for k, source in enumerate(sources):
        add_tiles(table, bounds[first + k], bounds[first + k + 1], adj, source, acc, masks)


def first_kernel(table, bounds, adj, *refs):
    *sources, acc, masks = refs
    set_masks(masks)
    acc[...] = jnp.zeros_like(acc)
    add_sources(table, bounds, adj, sources, 0, acc, masks)


def middle_kernel(table, bounds, adj, *refs):
    *sources, before, weights, acc, turned, masks = refs
    set_masks(masks)
    acc[...] = before[...]
    low = lax.broadcasted_iota(jnp.int32, (64, 128), 1) < 64
    for k in range(4):
        lanes = pl.multiple_of((lax.axis_index("yl") ^ (k >> 1)) * 128, 128)
        of_chip = weights[:, pl.ds(lanes, 128)].astype(jnp.float32)
        first = (lax.axis_index("core") ^ (k & 1)) == 0
        of_core = jnp.where(low == first, of_chip, pltpu.roll(of_chip, 64, 1))
        turned[k] = of_core.astype(turned.dtype)
    add_sources(table, bounds, adj, sources, 2, acc, masks)


def last_kernel(table, bounds, adj, *refs):
    *sources, before, features, weights, out, out_a, out_b, out_c, partial, acc, masks = refs
    outs = (out, out_a, out_b, out_c)
    lane = set_masks(masks)
    acc[...] = before[...]
    add_sources(table, bounds, adj, sources, 6, acc, masks)
    agg = [acc[r] + pltpu.roll(acc[r], 64, 1) for r in range(4)]
    rounded = jnp.concatenate([v.astype(jnp.bfloat16) for v in agg], axis=0)
    product = jnp.dot(features[...], rounded, preferred_element_type=jnp.float32)
    low = lax.broadcasted_iota(jnp.int32, (64, 128), 1) < 64
    for p in range(2):
        partial[:, p, :] = jnp.where(low, product[p * 128 : p * 128 + 64], product[p * 128 + 64 : p * 128 + 128])
    for r in range(2):
        packed = jnp.where(lane < 64, agg[r], agg[r + 2]).astype(out.dtype)
        for ref in outs:
            ref[pl.ds(r * 128, 128), :] = packed
    for k, ref in enumerate(outs):
        ref[pl.ds(256, 64), :] = weights[k]


def call(kernel, table, bounds, adj, sources, others, out_shape, keep_acc, name):
    smem = pl.BlockSpec(memory_space=pltpu.SMEM)
    vmem = pl.BlockSpec(memory_space=pltpu.VMEM)
    sources = [s.reshape(-1, 128, 128) for s in sources]
    return pl.pallas_call(
        kernel,
        out_shape=out_shape,
        in_specs=[smem, smem, vmem] + [vmem] * len(sources) + [vmem] * len(others),
        out_specs=jax.tree.map(lambda _: vmem, out_shape),
        scratch_shapes=([pltpu.VMEM((4, 128, 128), jnp.float32)] if keep_acc else []) + [
            pltpu.VMEM((3, 16, 128), jnp.bfloat16),
        ],
        compiler_params=pltpu.CompilerParams(vmem_limit_bytes=4 * 1024 * 1024),
        cost_estimate=pl.CostEstimate(flops=2 * 64 * 128 * 128 * 128, bytes_accessed=8 * 1024 * 1024, transcendentals=0),
        name=name,
    )(table, bounds, adj, *sources, *others)


def input_kernel(*refs):
    *messages, out = refs
    row = lax.broadcasted_iota(jnp.int32, (128, 128), 0)
    lane = lax.broadcasted_iota(jnp.int32, (128, 128), 1)
    factors = []
    for m in messages:
        block = m[pl.ds(256, 64), :].astype(jnp.float32)
        twice = jnp.concatenate([block, block], axis=0).T
        factors.append(jnp.where((row < 64) == (lane < 64), twice, 0.0).astype(jnp.bfloat16))
    sums = jnp.concatenate([m[pl.ds(0, 256), :] for m in messages], axis=1)
    result = lax.dot_general(
        jnp.concatenate(factors, axis=1), sums, (((1,), (1,)), ((), ())), preferred_element_type=jnp.float32
    )
    out[:, pl.ds(0, 256)] = result[:64].astype(out.dtype)
    out[:, pl.ds(256, 256)] = result[64:].astype(out.dtype)


def input_gradient(messages):
    vmem = pl.BlockSpec(memory_space=pltpu.VMEM)
    return pl.pallas_call(
        input_kernel,
        out_shape=jax.ShapeDtypeStruct((64, 512), jnp.bfloat16),
        in_specs=[vmem] * len(messages),
        out_specs=vmem,
        compiler_params=pltpu.CompilerParams(vmem_limit_bytes=4 * 1024 * 1024),
        cost_estimate=pl.CostEstimate(flops=2 * 128 * 512 * 256, bytes_accessed=400 * 1024, transcendentals=0),
        name="input_gradient",
    )(*messages)


def body(adj_tiles, tile_index, grad_out, relu_mask, features, weight):
    position = lax.axis_index(ROWS)
    source, place, half = where_held(tile_index[:, 1])
    low, high, position = gather_early(masked(grad_out, relu_mask), position)
    forwarded, others = gather_near(low, high)

    tables = tile_table(tile_index[:, 0] - position * 4, source, place, half, 8)
    f_rows = features.reshape(512, 64, 4).transpose(2, 1, 0).reshape(256, 512)
    low, high, tables, f_rows = lax.optimization_barrier((low, high, tables, f_rows))

    sums = jax.ShapeDtypeStruct((4, 128, 128), jnp.float32)
    acc = call(first_kernel, *tables, adj_tiles, [low, high], [], sums, False, "early_tiles")
    forwarded, acc = lax.optimization_barrier((forwarded, acc))
    far = gather_far(*forwarded)
    blocks = jax.ShapeDtypeStruct((4, 64, 128), jnp.bfloat16)
    acc, turned = call(middle_kernel, *tables, adj_tiles, forwarded + others, [acc, weight.T], (sums, blocks), False, "near_tiles")
    message = jax.ShapeDtypeStruct((320, 128), jnp.bfloat16)
    outs = (message, message, message, message, jax.ShapeDtypeStruct((64, 2, 128), jnp.float32))
    *messages, partial = call(last_kernel, *tables, adj_tiles, far, [acc, f_rows, turned], outs, True, "far_tiles")

    pieces = lax.all_to_all(partial, ROWS, 0, 0, tiled=True)
    arrived = messages[:1] + [lax.ppermute(m, SLAB, pairs) for m, pairs in zip(messages[1:], FLIPS)]
    grad_input = input_gradient(arrived).T
    total = jnp.sum(pieces, axis=0)
    grad_weight = jnp.concatenate([total[p : p + 1, k : k + 64] for p in range(2) for k in (0, 64)], axis=0)
    return grad_input, grad_weight


def solution(mesh):
    fine = Mesh(mesh.devices.reshape(NZ, NY, NX, NL, NC), ALL)
    return jax.shard_map(
        body,
        mesh=fine,
        in_specs=(P(ROWS, None, None), P(ROWS, None), P(ROWS, SLAB), P(ROWS, SLAB), P(ROWS, None), P(None, SLAB)),
        out_specs=(P(ROWS, SLAB), P(ROWS, SLAB)),
        check_vma=False,
    )
```
